32 devices in a mesh: dp: 4 (over y, x), expert: 8 (over z, core).
Axes of the slice: x: 2, y: 2, z: 4, core: 2. Of those that a mesh axis runs over, the one named last changes fastest.
Arguments:
- tokens: bfloat16 [4096, 2048], P(('dp', 'expert')), may hold values from -6 to 6
- cotangent: bfloat16 [4096, 2048], P(('dp', 'expert')), may hold values from -1.5 to 1.5
- probs: bfloat16 [4096, 2], P(('dp', 'expert')), may hold values from 0.099609375 to 1
- expert_ids: int32 [4096, 2], P(('dp', 'expert')), may hold values from 0 to 7, all different within a row; in each aligned block of 128 rows (0 to 127, 128 to 255, ...) at most 64 rows name the same one
- holder: int32 [8], replicated, may hold values from 0 to 7, each once
- partner: int32 [8], replicated, may hold values from 0 to 7, as said below
- w_gate: bfloat16 [8, 2048, 768], P('expert', 'dp'), may hold values from -0.125 to 0.125
- w_up: bfloat16 [8, 2048, 768], P('expert', 'dp'), may hold values from -0.125 to 0.125
- w_down: bfloat16 [8, 768, 2048], P('expert', None, 'dp'), may hold values from -0.21875 to 0.21875
Outputs:
- grad_tokens: bfloat16 [4096, 2048], P(('dp', 'expert'))
- grad_probs: bfloat16 [4096, 2], P(('dp', 'expert'))
- grad_gate: bfloat16 [8, 2048, 768], P('expert', 'dp')
- grad_up: bfloat16 [8, 2048, 768], P('expert', 'dp')
- grad_down: bfloat16 [8, 768, 2048], P('expert', None, 'dp')
The draws below stay inside these ranges and needn't reach their ends.
Inputs may be any that keep to these rules, and one draw needn't show every extreme that they name: `expert_ids`: within each aligned block of 128 token rows (the rows of one device), no expert is named by more than 64 token-pick pairs, a bound that some block reaches; a row names 2 different experts. `holder`: every expert once. A perfect matching: partner[partner[j]] = j and partner[j] != j.
All inputs are finite; a program needn't handle non-finite values.
Results may differ from the reference program's by a relative error of at most 0.013.
Values may be sent and summed in bfloat16 or wider, within the bound.
No kernel may reach another device: no remote copies, remote signals or barrier semaphores. Data moves between devices by JAX's collectives and lax.ppermute only.
A program may use at most 128 MiB of HBM per device.

```python
import math
import jax
import jax.numpy as jnp
import numpy as np
from jax import lax

D = 2048
FF = 768
TOPK = 2
TOK_DEV = 128
EXPERTS = 8
CAP = 64
TOKENS = 4096
N_DP = 4
N_EXPERT = 8


def draw_partner(key, part):
    order = jax.random.permutation(key, EXPERTS).astype(jnp.int32)
    firsts = order[0::2]
    seconds = order[1::2]
    result = jnp.zeros((EXPERTS,), jnp.int32).at[firsts].set(seconds).at[seconds].set(firsts)
    return result.astype(jnp.int32)


def block_levels(own_key, shape, pieces, low, high):
    level = 1.0
    for axis_at, shards_of in pieces:
        draws = jax.random.uniform(jax.random.fold_in(jax.random.fold_in(own_key, 6), axis_at), (shards_of,), jnp.float32, low / len(pieces), high / len(pieces))
        level = level * jnp.repeat(jnp.exp(draws), shape[axis_at] // shards_of).reshape((-1,) + (1,) * (len(shape) - 1 - axis_at))
    return level


def routed_block(own_key, own, number, rows, amount, top, bound, skew):
    ranking = jax.random.permutation(own_key, amount)
    packed, ordinary = portions_of(amount, rows * top, bound, skew, True), portions_of(amount, rows * top, bound, skew, False)
    places = jnp.arange(amount)

    def named(lengths, offset_by):
        used = int((lengths > 0).sum())
        fixed = max(1, used // 4)
        shifted = fixed + (places - fixed + offset_by * (used - fixed)) % max(1, amount - fixed)
        return jnp.zeros((amount,), jnp.int32).at[ranking[jnp.where(places < fixed, places, shifted)]].set(jnp.asarray(lengths, jnp.int32))

    lengths = jnp.where(number % 4 == 0, named(packed, number // 4), named(ordinary, number - number // 4 - 1))
    mixed = jax.random.permutation(jax.random.fold_in(own, 3), amount)
    source_of, sink = mixed[0:amount // 2 * 2:2], mixed[1:amount // 2 * 2:2]
    room = jnp.minimum(lengths[source_of] - 1, bound - lengths[sink]) // 2
    room = jnp.where((source_of == ranking[0]) | (sink == ranking[0]) | (lengths[sink] == 0), 0, jnp.maximum(room, 0))
    shifted = jax.random.randint(jax.random.fold_in(own, 4), (amount // 2,), 0, 1 << 20) % (room + 1)
    lengths = lengths.at[source_of].add(-shifted).at[sink].add(shifted)
    items = jnp.searchsorted(jnp.cumsum(lengths), jnp.arange(rows * top), side="right").astype(jnp.int32)
    listing = items.reshape(top, rows).T
    listing = listing[jax.random.permutation(jax.random.fold_in(own, 1), rows)]
    offset_by = jax.random.randint(jax.random.fold_in(own, 2), (rows, 1), 0, top)
    return jnp.take_along_axis(listing, (jnp.arange(top)[None, :] + offset_by) % top, axis=1)


def portions_of(number_of, total, reach, lean, full):
    loads = [(1 << 20) // math.isqrt(standing ** lean) + 1 for standing in range(1, number_of + 1)]
    largest = reach if full else min(reach, max(-(-total // number_of), total * loads[0] // sum(loads)))
    least = 1 if total - largest >= number_of - 1 else 0
    counts, spare = [largest] + [least] * (number_of - 1), total - largest - least * (number_of - 1)
    while spare > 0:
        free = [i for i in range(1, number_of) if counts[i] < largest] or [i for i in range(1, number_of) if counts[i] < reach]
        whole, left = sum([loads[i] for i in free]), spare
        for i in free:
            more = min(reach - counts[i], max(1, left * loads[i] // whole), spare)
            counts[i] = counts[i] + more
            spare = spare - more
    return np.array(counts)


def centred(own_key, dims, deviation, reach, split=(), kind=jnp.bfloat16):
    gain = block_levels(own_key, dims, split, -0.22, 0.18) if split else 1.0
    values = jax.random.normal(own_key, dims, jnp.float32) * deviation * gain
    return jnp.minimum(jnp.maximum(values, -reach), reach).astype(kind)


def setup_inputs(seed: int = 0) -> dict:
    splits = jax.random.split(jax.random.key(seed), 10)
    tokens = centred(splits[0], (TOKENS, D), 1.0, 6.0, ((0, 32),))
    cotangent = centred(splits[1], (TOKENS, D), 0.25, 1.5, ((0, 32),))
    probs = jnp.clip(jnp.exp(math.log(1.0) - 2.306499 * jax.random.uniform(splits[2], (TOKENS, TOPK), jnp.float32) ** block_levels(splits[2], (TOKENS, TOPK), ((0, 32),), -0.2, 0.2)), 0.099609375, 1.0).astype(jnp.bfloat16)
    expert_ids_keys = jax.random.split(jax.random.fold_in(splits[3], 1), TOKENS // TOK_DEV)
    expert_ids_turns = jax.random.permutation(jax.random.fold_in(splits[3], 3), TOKENS // TOK_DEV)
    expert_ids = jax.vmap(lambda own, number: routed_block(jax.random.fold_in(splits[3], 2), own, number, TOK_DEV, EXPERTS, TOPK, CAP, 2))(expert_ids_keys, expert_ids_turns).reshape((TOKENS, TOPK))
    holder = jax.random.permutation(splits[4], EXPERTS).astype(jnp.int32)
    partner = draw_partner(jax.random.fold_in(splits[9], 71), 0)
    w_gate = centred(splits[6], (EXPERTS, D, FF), D ** -0.5, 0.125, ((0, 8), (1, 4)))
    w_up = centred(splits[7], (EXPERTS, D, FF), D ** -0.5, 0.125, ((0, 8), (1, 4)))
    w_down = centred(splits[8], (EXPERTS, FF, D), FF ** -0.5, 0.21875, ((0, 8), (2, 4)))
    return dict(tokens=tokens, cotangent=cotangent, probs=probs, expert_ids=expert_ids, holder=holder, partner=partner, w_gate=w_gate, w_up=w_up, w_down=w_down)


def expert_pass(rows_x, rows_dy, rows_p, gate_w, up_w, down_w):
    x_wide = rows_x.astype(jnp.float32)
    gate_pre = jnp.dot(x_wide, gate_w.astype(jnp.float32))
    up_pre = jnp.dot(x_wide, up_w.astype(jnp.float32))
    gate_sig = jax.nn.sigmoid(gate_pre)
    hidden = (gate_pre * gate_sig * up_pre).astype(jnp.bfloat16)
    expert_out = jnp.dot(hidden.astype(jnp.float32), down_w.astype(jnp.float32)).astype(jnp.bfloat16)
    scaled = (rows_p.astype(jnp.float32)[:, None] * rows_dy.astype(jnp.float32)).astype(jnp.bfloat16)
    d_hidden = jnp.dot(scaled.astype(jnp.float32), down_w.astype(jnp.float32).T)
    d_gate = (d_hidden * up_pre * gate_sig * (1.0 + gate_pre * (1.0 - gate_sig))).astype(jnp.bfloat16)
    d_up = (d_hidden * gate_pre * gate_sig).astype(jnp.bfloat16)
    pair_grad = (jnp.dot(d_gate.astype(jnp.float32), gate_w.astype(jnp.float32).T)
                 + jnp.dot(d_up.astype(jnp.float32), up_w.astype(jnp.float32).T)).astype(jnp.bfloat16)
    score = jnp.sum(rows_dy.astype(jnp.float32) * expert_out.astype(jnp.float32), axis=1)
    return hidden, scaled, d_gate, d_up, pair_grad, score


def group_sum(left, right, part):
    total = jnp.zeros((left.shape[1], right.shape[1]), jnp.float32)
    for group in range(N_DP):
        lower = group * part
        piece = jnp.dot(left[lower:lower + part].astype(jnp.float32).T, right[lower:lower + part].astype(jnp.float32))
        rounded = lax.optimization_barrier(piece.astype(jnp.bfloat16))
        total = total + rounded.astype(jnp.float32)
    return total.astype(jnp.bfloat16)


def reference(tokens, cotangent, probs, expert_ids, holder, partner, w_gate, w_up, w_down):
    groups = N_DP * N_EXPERT
    pair_count = TOK_DEV * TOPK
    flat_ids = expert_ids.reshape(groups, pair_count)
    numbers = jnp.arange(EXPERTS, dtype=jnp.int32)
    onehot = (flat_ids[:, :, None] == numbers[None, None, :]).astype(jnp.int32)
    earlier = jnp.cumsum(onehot, axis=1) - onehot
    slot_index = jnp.sum(earlier * onehot, axis=2).astype(jnp.int32)
    group_ids = jnp.arange(groups, dtype=jnp.int32)[:, None]
    position = ((flat_ids * groups + group_ids) * CAP + slot_index).astype(jnp.int32)
    pair_ids = jnp.arange(TOKENS * TOPK, dtype=jnp.int32)
    empty_pair = TOKENS * TOPK
    pair_table = jnp.full((EXPERTS * groups * CAP,), empty_pair, jnp.int32).at[position.reshape(-1)].set(pair_ids)
    pair_table = pair_table.reshape(EXPERTS, groups * CAP)
    token_table = (pair_table // TOPK).astype(jnp.int32)
    zero_row = jnp.zeros((1, D), jnp.bfloat16)
    x_ext = jnp.concatenate([tokens, zero_row], axis=0)
    dy_ext = jnp.concatenate([cotangent, zero_row], axis=0)
    p_ext = jnp.concatenate([probs.reshape(-1), jnp.zeros((1,), jnp.bfloat16)], axis=0)
    home_slot = jnp.argsort(holder).astype(jnp.int32)
    part = N_EXPERT * CAP

    def one_expert(carry, expert):
        grad_acc, score_acc = carry
        pair_rows = pair_table[expert]
        token_rows = token_table[expert]
        rows_x = x_ext[token_rows]
        rows_dy = dy_ext[token_rows]
        rows_p = p_ext[pair_rows]
        where = home_slot[expert]
        hidden, scaled, d_gate, d_up, pair_grad, score = expert_pass(
            rows_x, rows_dy, rows_p, w_gate[where], w_up[where], w_down[where])
        grad_acc = grad_acc.at[token_rows].add(pair_grad.astype(jnp.float32))
        score_acc = score_acc.at[pair_rows].set(score)
        grads = (group_sum(rows_x, d_gate, part), group_sum(rows_x, d_up, part), group_sum(hidden, scaled, part))
        return (grad_acc, score_acc), grads

    start = (jnp.zeros((TOKENS + 1, D), jnp.float32), jnp.zeros((TOKENS * TOPK + 1,), jnp.float32))
    (grad_acc, score_acc), (all_gate, all_up, all_down) = lax.scan(one_expert, start, numbers)
    grad_tokens = grad_acc[:TOKENS].astype(jnp.bfloat16)
    grad_probs = score_acc[:TOKENS * TOPK].reshape(TOKENS, TOPK).astype(jnp.bfloat16)
    after = holder[partner]
    return grad_tokens, grad_probs, all_gate[after], all_up[after], all_down[after]
```

```python
import jax
import jax.numpy as jnp
from jax import lax
from jax.experimental import pallas as pl
from jax.experimental.pallas import tpu as pltpu
from jax.sharding import PartitionSpec as P

BF = jnp.bfloat16
F32 = jnp.float32


def contract(left, right, dim_left, dim_right):
    return lax.dot_general(
        left, right, (((dim_left,), (dim_right,)), ((), ())), preferred_element_type=F32
    )


def matchings(size):
    def pairs_of(left):
        if not left:
            yield []
            return
        for other in left[1:]:
            rest = [one for one in left[1:] if one != other]
            for tail in pairs_of(rest):
                yield [(left[0], other)] + tail

    tables = []
    for pairs in pairs_of(list(range(size))):
        table = [0] * size
        for a, b in pairs:
            table[a], table[b] = b, a
        tables.append(table)
    return tables


def dp_swap(value, bit):
    count = lax.axis_size("dp")
    return lax.ppermute(value, "dp", [(i, i ^ bit) for i in range(count)])


def core_swap(value):
    count = lax.axis_size("expert")
    return lax.ppermute(value, "expert", [(i, i ^ 1) for i in range(count)])


def chip_shift(value, step):
    count = lax.axis_size("expert")
    return lax.ppermute(value, "expert", [(i, (i + 2 * step) % count) for i in range(count)])


CHUNKS = (((1, 0), (3, 0)), ((2, 1), (3, 1)), ((0, 0), (2, 0)), ((0, 1), (1, 1)))
BLOCKS = tuple(key for chunk in CHUNKS for key in chunk)
LANES = 128
VMEM_LIMIT = 48 * 1024 * 1024
SMEM_SPEC = pl.BlockSpec(memory_space=pltpu.SMEM)
VMEM_SPEC = pl.BlockSpec(memory_space=pltpu.VMEM)
ANY_SPEC = pl.BlockSpec(memory_space=pl.ANY)


def shape_of(*dims, dtype=BF):
    return jax.ShapeDtypeStruct(dims, dtype)


def pack(place, holder, tokens, cotangent, probs, expert_ids, w_gate, w_up, w_down):
    rows, depth = tokens.shape
    span = holder.shape[0]
    tile, ff = w_gate.shape
    block = depth // 8

    def kernel(place_ref, holder_ref, x_ref, dy_ref, p_ref, id_ref, g_ref, u_ref, d_ref, w_out, r_out):
        w_out[:, :ff] = g_ref[...]
        w_out[:, ff : 2 * ff] = u_ref[...]
        w_out[:, 2 * ff :] = d_ref[...].T
        here = place_ref[0]
        for at, (quarter, half) in enumerate(BLOCKS):
            start = pl.multiple_of(((here ^ quarter) * 2 + half) * block, block)
            r_out[:, at * block : (at + 1) * block] = x_ref[:, pl.ds(start, block)]
            r_out[:, depth + at * block : depth + (at + 1) * block] = dy_ref[:, pl.ds(start, block)]
        lanes = lax.broadcasted_iota(jnp.int32, (rows, LANES), 1)
        share = jnp.zeros((rows, LANES), F32)
        for pick in range(p_ref.shape[1]):
            chosen = id_ref[:, pick : pick + 1]
            value = p_ref[:, pick : pick + 1].astype(F32)
            for slot in range(span):
                hit = (lanes == slot) & (chosen == holder_ref[slot])
                share = jnp.where(hit, value, share)
        r_out[:, 2 * depth :] = share.astype(BF)

    return pl.pallas_call(
        kernel,
        out_shape=[shape_of(tile, 3 * ff), shape_of(rows, 2 * depth + LANES)],
        in_specs=[SMEM_SPEC] * 2 + [VMEM_SPEC] * 7,
        out_specs=[VMEM_SPEC] * 2,
        compiler_params=pltpu.CompilerParams(vmem_limit_bytes=VMEM_LIMIT),
        name="pack",
    )(place, holder, tokens, cotangent, probs, expert_ids, w_gate, w_up, w_down)


def gather_tiles(tile):
    half = tile.shape[0] // 2
    from_x = dp_swap(tile, 1)
    from_y = dp_swap(tile, 2)
    return tile, from_x, from_y, dp_swap(from_x[:half], 2), dp_swap(from_y[half:], 1)


def block_source(tiles, key, half):
    own, from_x, from_y, far_low, far_high = tiles
    quarter, side = key
    if quarter == 3:
        return (far_high if side else far_low), 0
    return (own, from_x, from_y)[quarter], side * half


def gather_rows(block):
    chips = lax.axis_size("expert") // 2
    own = [block]
    for _ in range(chips - 1):
        own.append(chip_shift(own[-1], 1))
    return own + [core_swap(one) for one in own]


def start_all(copies):
    for copy in copies:
        copy.start()


def wait_all(copies):
    for copy in copies:
        copy.wait()


def my_weight(shares, index):
    lanes = lax.broadcasted_iota(jnp.int32, shares.shape, 1)
    return jnp.sum(jnp.where(lanes == index, shares.astype(F32), 0.0), axis=1, keepdims=True)


def forward(index, parts, tiles, depth, ff):
    count = len(parts)
    rows = parts[0].shape[0]
    total = count * rows
    half = tiles[0].shape[0] // 2
    width = depth // 4
    group = 2 * rows
    groups = total // group
    n_tiles = len(tiles)

    def kernel(*refs):
        index_ref = refs[0]
        part_refs = refs[1 : 1 + count]
        tile_refs = refs[1 + count : 1 + count + n_tiles]
        (x_out, dy_out, w_out, hid_out, hw_out, fg_out, fu_out, sx_out, sy_out) = refs[
            1 + count + n_tiles : 10 + count + n_tiles
        ]
        x_s, dy_s, share_s, w_s, sem_w, sem_x, sem_s, sem_dy, sem_out = refs[10 + count + n_tiles :]
        w_copies = []
        for at, key in enumerate(BLOCKS):
            source, first = block_source(tile_refs, key, half)
            w_copies.append(
                pltpu.make_async_copy(
                    source.at[pl.ds(first, half), pl.ds(0, 2 * ff)],
                    w_s.at[pl.ds(at * half, half)],
                    sem_w.at[at],
                )
            )
        x_copies, s_copies, dy_copies = [], [], []
        for at in range(count):
            place = pl.ds(at * rows, rows)
            x_copies.append(
                pltpu.make_async_copy(
                    part_refs[at].at[:, pl.ds(0, depth)], x_s.at[place], sem_x.at[at]
                )
            )
            s_copies.append(
                pltpu.make_async_copy(
                    part_refs[at].at[:, pl.ds(2 * depth, LANES)], share_s.at[place], sem_s.at[at]
                )
            )
            dy_copies.append(
                pltpu.make_async_copy(
                    part_refs[at].at[:, pl.ds(depth, depth)], dy_s.at[place], sem_dy.at[at]
                )
            )
        start_all(w_copies)
        start_all(x_copies)
        start_all(s_copies)
        start_all(dy_copies)
        wait_all(w_copies)
        wait_all(x_copies)
        wait_all(s_copies)
        out_copies = [
            pltpu.make_async_copy(x_s, x_out, sem_out.at[0]),
            pltpu.make_async_copy(w_s, w_out, sem_out.at[1]),
            pltpu.make_async_copy(dy_s, dy_out, sem_out.at[2]),
        ]
        start_all(out_copies[:2])
        index = index_ref[0]

        def step(at, carry):
            place = pl.ds(pl.multiple_of(at * group, group), group)
            both = jnp.dot(x_s[place, :], w_s[...], preferred_element_type=F32)
            gate, up = both[:, :ff], both[:, ff:]
            sig = jax.nn.sigmoid(gate)
            act = gate * sig
            hid = (act * up).astype(BF)
            hid_out[place, :] = hid
            hw_out[place, :] = (hid.astype(F32) * my_weight(share_s[place, :], index)).astype(BF)
            fg_out[place, :] = (up * sig * (1.0 + gate * (1.0 - sig))).astype(BF)
            fu_out[place, :] = act.astype(BF)
            return carry

        lax.fori_loop(0, groups, step, 0)
        wait_all(dy_copies)
        out_copies[2].start()
        sx_out[...] = contract(hw_out[...], dy_s[:, :width], 0, 0).astype(BF)
        sy_out[...] = contract(hw_out[...], dy_s[:, width : 2 * width], 0, 0).astype(BF)
        wait_all(out_copies)

    return pl.pallas_call(
        kernel,
        out_shape=[
            shape_of(total, depth),
            shape_of(total, depth),
            shape_of(depth, 2 * ff),
            shape_of(total, ff),
            shape_of(total, ff),
            shape_of(total, ff),
            shape_of(total, ff),
            shape_of(ff, width),
            shape_of(ff, width),
        ],
        in_specs=[SMEM_SPEC] + [ANY_SPEC] * (count + n_tiles),
        out_specs=[ANY_SPEC] * 3 + [VMEM_SPEC] * 6,
        scratch_shapes=[
            pltpu.VMEM((total, depth), BF),
            pltpu.VMEM((total, depth), BF),
            pltpu.VMEM((total, LANES), BF),
            pltpu.VMEM((depth, 2 * ff), BF),
            pltpu.SemaphoreType.DMA((len(BLOCKS),)),
            pltpu.SemaphoreType.DMA((count,)),
            pltpu.SemaphoreType.DMA((count,)),
            pltpu.SemaphoreType.DMA((count,)),
            pltpu.SemaphoreType.DMA((3,)),
        ],
        compiler_params=pltpu.CompilerParams(vmem_limit_bytes=VMEM_LIMIT),
        name="forward",
    )(index, *parts, *tiles)


def backward(index, parts, tiles, x, dy, hid, fg, fu):
    count = len(parts)
    rows = parts[0].shape[0]
    total, depth = x.shape
    ff = hid.shape[1]
    half = tiles[0].shape[0] // 2
    width = depth // 4
    group = 2 * rows
    groups = total // group
    n_tiles = len(tiles)

    def kernel(*refs):
        index_ref = refs[0]
        part_refs = refs[1 : 1 + count]
        tile_refs = refs[1 + count : 1 + count + n_tiles]
        rest = refs[1 + count + n_tiles :]
        x_ref, dy_ref, hid_ref, fg_ref, fu_ref, d_out, score_out, sx_out, sy_out = rest[:9]
        share_s, w_s, x_s, sem_s, sem_w, sem_x = rest[9:]
        w_copies = []
        for at, key in enumerate(BLOCKS):
            source, first = block_source(tile_refs, key, half)
            w_copies.append(
                pltpu.make_async_copy(
                    source.at[pl.ds(first, half), pl.ds(2 * ff, ff)],
                    w_s.at[pl.ds(at * half, half)],
                    sem_w.at[at],
                )
            )
        s_copies = []
        for at in range(count):
            s_copies.append(
                pltpu.make_async_copy(
                    part_refs[at].at[:, pl.ds(2 * depth, LANES)],
                    share_s.at[pl.ds(at * rows, rows)],
                    sem_s.at[at],
                )
            )
        x_copy = pltpu.make_async_copy(x_ref.at[:, pl.ds(0, 2 * width)], x_s, sem_x)
        start_all(w_copies)
        start_all(s_copies)
        x_copy.start()
        wait_all(w_copies)
        wait_all(s_copies)
        index = index_ref[0]

        def step(at, carry):
            place = pl.ds(pl.multiple_of(at * group, group), group)
            plain = jnp.dot(dy_ref[place, :], w_s[...], preferred_element_type=F32)
            score = jnp.sum(hid_ref[place, :].astype(F32) * plain, axis=1, keepdims=True)
            score_out[place, :] = score
            d_hidden = plain * my_weight(share_s[place, :], index)
            d_out[place, :ff] = (d_hidden * fg_ref[place, :].astype(F32)).astype(BF)
            d_out[place, ff:] = (d_hidden * fu_ref[place, :].astype(F32)).astype(BF)
            return carry

        lax.fori_loop(0, groups, step, 0)
        x_copy.wait()
        sx_out[...] = contract(x_s[:, :width], d_out[...], 0, 0).astype(BF)
        sy_out[...] = contract(x_s[:, width:], d_out[...], 0, 0).astype(BF)

    return pl.pallas_call(
        kernel,
        out_shape=[
            shape_of(total, 2 * ff),
            shape_of(total, 1, dtype=F32),
            shape_of(width, 2 * ff),
            shape_of(width, 2 * ff),
        ],
        in_specs=[SMEM_SPEC] + [ANY_SPEC] * (count + n_tiles + 1) + [VMEM_SPEC] * 4,
        out_specs=[VMEM_SPEC] * 4,
        scratch_shapes=[
            pltpu.VMEM((total, LANES), BF),
            pltpu.VMEM((depth, ff), BF),
            pltpu.VMEM((total, 2 * width), BF),
            pltpu.SemaphoreType.DMA((count,)),
            pltpu.SemaphoreType.DMA((len(BLOCKS),)),
            pltpu.SemaphoreType.DMA,
        ],
        compiler_params=pltpu.CompilerParams(vmem_limit_bytes=VMEM_LIMIT),
        name="backward",
    )(index, *parts, *tiles, x, dy, hid, fg, fu)


def unpack_rows(place, value):
    rows, depth = value.shape
    block = depth // 8

    def kernel(place_ref, v_ref, out_ref):
        here = place_ref[0]
        for at, (quarter, half) in enumerate(BLOCKS):
            start = pl.multiple_of(((here ^ quarter) * 2 + half) * block, block)
            out_ref[:, pl.ds(start, block)] = v_ref[:, at * block : (at + 1) * block]

    return pl.pallas_call(
        kernel,
        out_shape=shape_of(rows, depth),
        in_specs=[SMEM_SPEC, VMEM_SPEC],
        out_specs=VMEM_SPEC,
        compiler_params=pltpu.CompilerParams(vmem_limit_bytes=VMEM_LIMIT),
        name="unpack_rows",
    )(place, value)


def reduce_chunks(send_x, send_y, keep_low, keep_high, axis):
    got_x = dp_swap(send_x, 1)
    got_y = dp_swap(send_y, 2)
    sum_low = keep_low + got_x.astype(F32)
    sum_high = keep_high + got_y.astype(F32)
    half = sum_low.shape[axis] // 2
    near = lambda v: lax.slice_in_dim(v, 0, half, axis=axis)
    far = lambda v: lax.slice_in_dim(v, half, 2 * half, axis=axis)
    low = near(sum_low) + dp_swap(far(sum_low).astype(BF), 2).astype(F32)
    high = near(sum_high) + dp_swap(far(sum_high).astype(BF), 1).astype(F32)
    return jnp.concatenate([low.astype(BF), high.astype(BF)], axis=axis)


def gathered(tokens, cotangent, probs, expert_ids, holder, partner, w_gate, w_up, w_down):
    span = lax.axis_size("expert")
    chips = span // 2
    rows, depth = tokens.shape
    ff = w_gate.shape[2]
    width = depth // 4
    place = lax.axis_index("dp")[None].astype(jnp.int32)
    index = lax.axis_index("expert").astype(jnp.int32)
    chip, core = index // 2, index % 2

    tile, packed = pack(
        place, holder, tokens, cotangent, probs, expert_ids, w_gate[0], w_up[0], w_down[0]
    )
    tiles = gather_tiles(tile)
    parts = gather_rows(packed)
    x, dy, gate_up, hid, weighted, fg, fu, send_x, send_y = forward(
        index[None], parts, tiles, depth, ff
    )
    column = lambda v, c: v[:, c * width : (c + 1) * width]
    down_sum = reduce_chunks(
        send_x,
        send_y,
        contract(weighted, column(dy, 2), 0, 0),
        contract(weighted, column(dy, 3), 0, 0),
        1,
    )
    d_both, score, send_x, send_y = backward(index[None], parts, tiles, x, dy, hid, fg, fu)
    both_sum = reduce_chunks(
        send_x,
        send_y,
        contract(column(x, 2), d_both, 0, 0),
        contract(column(x, 3), d_both, 0, 0),
        0,
    )

    row_grad = contract(d_both, gate_up, 1, 1).astype(BF)
    near, away = row_grad[: chips * rows], row_grad[chips * rows :]
    both = (near.astype(F32) + core_swap(away).astype(F32)).astype(BF)
    pieces = [both[s * rows : (s + 1) * rows] for s in range(chips)]
    total = pieces[-1]
    for s in range(chips - 2, -1, -1):
        total = (pieces[s].astype(F32) + chip_shift(total, -1).astype(F32)).astype(BF)
    grad_tokens = unpack_rows(place, total)

    steps = jnp.arange(chips, dtype=jnp.int32)
    own_chips = (chip - steps) % chips
    order = jnp.concatenate([2 * own_chips + core, 2 * own_chips + 1 - core])
    everyone = jnp.arange(span, dtype=jnp.int32)
    back = jnp.sum((order[None, :] == everyone[:, None]) * everyone[None, :], axis=1)
    by_device = jnp.take(score.reshape(span, rows), back, axis=0)
    got = lax.all_to_all(by_device, "expert", split_axis=0, concat_axis=0, tiled=True)
    hits = expert_ids[:, :, None] == holder[None, None, :]
    picked = jnp.sum(jnp.where(hits, got.T[:, None, :], 0.0), axis=2)
    grad_probs = picked.astype(BF)

    tables = matchings(span)
    chosen = jnp.argmax(jnp.all(jnp.array(tables, jnp.int32) == partner[None, :], axis=1))

    def trade(table):
        return lambda v: lax.ppermute(v, "expert", list(enumerate(table)))

    branches = [trade(table) for table in tables]
    grad_down = lax.switch(chosen, branches, down_sum)
    both_sum = lax.switch(chosen, branches, both_sum)
    grad_gate, grad_up = both_sum[:, :ff], both_sum[:, ff:]
    return grad_tokens, grad_probs, grad_gate[None], grad_up[None], grad_down[None]


def contract_last(left, right):
    return lax.dot_general(
        left, right, (((1,), (1,)), ((), ())), preferred_element_type=jnp.float32
    )


def contract_first(left, right):
    return lax.dot_general(
        left, right, (((0,), (0,)), ((), ())), preferred_element_type=jnp.float32
    )


def move_weights(gate_tile, up_tile, down_tile, partner):
    spread = (
        lax.all_to_all(gate_tile, "expert", split_axis=1, concat_axis=0, tiled=True),
        lax.all_to_all(up_tile, "expert", split_axis=1, concat_axis=0, tiled=True),
        lax.all_to_all(down_tile, "expert", split_axis=1, concat_axis=0, tiled=True),
    )
    chosen = [jnp.take(piece, partner, axis=0) for piece in spread]
    return (
        lax.all_to_all(chosen[0], "expert", split_axis=0, concat_axis=1, tiled=True),
        lax.all_to_all(chosen[1], "expert", split_axis=0, concat_axis=1, tiled=True),
        lax.all_to_all(chosen[2], "expert", split_axis=0, concat_axis=1, tiled=True),
    )


def shards(tokens, cotangent, probs, expert_ids, holder, partner, w_gate, w_up, w_down):
    experts = holder.shape[0]
    span_size = lax.axis_size("expert")
    tok_rows, picks = expert_ids.shape
    pair_count = tok_rows * picks
    capacity = 2 * pair_count // experts
    numbers = jnp.arange(experts, dtype=jnp.int32)
    holder_hits = (holder[None, :] == numbers[:, None]).astype(jnp.int32)
    home_slot = jnp.sum(holder_hits * numbers[None, :], axis=1)
    gate_tile, up_tile, down_tile = move_weights(w_gate, w_up, w_down, partner)
    partner_hits = (home_slot[:, None] == numbers[None, :]).astype(jnp.int32)
    target = jnp.sum(partner_hits * partner[None, :], axis=1)
    full_gate, full_up, full_down = (
        lax.all_gather(gate_tile, "dp", axis=1, tiled=True),
        lax.all_gather(up_tile, "dp", axis=1, tiled=True),
        lax.all_gather(down_tile, "dp", axis=2, tiled=True),
    )
    gate_w = full_gate[0]
    up_w = full_up[0]
    down_w = full_down[0]
    flat_ids = expert_ids.reshape(pair_count)
    onehot = (flat_ids[:, None] == numbers[None, :]).astype(jnp.int32)
    earlier = jnp.cumsum(onehot, axis=0) - onehot
    slot_index = jnp.sum(earlier * onehot, axis=1)
    dest_dev = jnp.sum(onehot * target[None, :], axis=1)
    pair_row = dest_dev * capacity + slot_index
    row_table = (
        jnp.full((span_size * capacity,), pair_count, jnp.int32)
        .at[pair_row]
        .set(jnp.arange(pair_count, dtype=jnp.int32))
    )
    token_of_row = row_table // picks
    zero_row = jnp.zeros((1, tokens.shape[1]), jnp.bfloat16)
    send_x = jnp.concatenate([tokens, zero_row], axis=0)[token_of_row]
    send_dy = jnp.concatenate([cotangent, zero_row], axis=0)[token_of_row]
    send_p = jnp.concatenate([probs.reshape(pair_count), jnp.zeros((1,), jnp.bfloat16)], axis=0)[
        row_table
    ]
    send_scaled = (send_p.astype(jnp.float32)[:, None] * send_dy.astype(jnp.float32)).astype(
        jnp.bfloat16
    )
    recv_x, scaled = (
        lax.all_to_all(send_x, "expert", split_axis=0, concat_axis=0, tiled=True),
        lax.all_to_all(send_scaled, "expert", split_axis=0, concat_axis=0, tiled=True),
    )
    gate_pre = jnp.dot(recv_x, gate_w, preferred_element_type=jnp.float32)
    up_pre = jnp.dot(recv_x, up_w, preferred_element_type=jnp.float32)
    gate_sig = jax.nn.sigmoid(gate_pre)
    hidden = (gate_pre * gate_sig * up_pre).astype(jnp.bfloat16)
    expert_out = jnp.dot(hidden, down_w, preferred_element_type=jnp.float32).astype(jnp.bfloat16)
    d_hidden = contract_last(scaled, down_w)
    d_gate = (d_hidden * up_pre * gate_sig * (1.0 + gate_pre * (1.0 - gate_sig))).astype(
        jnp.bfloat16
    )
    d_up = (d_hidden * gate_pre * gate_sig).astype(jnp.bfloat16)
    pair_grad = (contract_last(d_gate, gate_w) + contract_last(d_up, up_w)).astype(jnp.bfloat16)
    back_out, back_grad = (
        lax.all_to_all(expert_out, "expert", split_axis=0, concat_axis=0, tiled=True),
        lax.all_to_all(pair_grad, "expert", split_axis=0, concat_axis=0, tiled=True),
    )
    row_score = jnp.sum(send_dy.astype(jnp.float32) * back_out.astype(jnp.float32), axis=1).astype(
        jnp.bfloat16
    )
    grad_probs = row_score[pair_row].reshape(tok_rows, picks)
    picked_rows = back_grad[pair_row].reshape(tok_rows, picks, back_grad.shape[1])
    grad_tokens = jnp.sum(picked_rows.astype(jnp.float32), axis=1).astype(jnp.bfloat16)
    shares = (
        lax.psum_scatter(
            contract_first(recv_x, d_gate)[None].astype(jnp.bfloat16),
            "dp",
            scatter_dimension=1,
            tiled=True,
        ).astype(jnp.float32),
        lax.psum_scatter(
            contract_first(recv_x, d_up)[None].astype(jnp.bfloat16),
            "dp",
            scatter_dimension=1,
            tiled=True,
        ).astype(jnp.float32),
        lax.psum_scatter(
            contract_first(hidden, scaled)[None].astype(jnp.bfloat16),
            "dp",
            scatter_dimension=2,
            tiled=True,
        ).astype(jnp.float32),
    )
    grad_gate = shares[0].astype(jnp.bfloat16)
    grad_up = shares[1].astype(jnp.bfloat16)
    grad_down = shares[2].astype(jnp.bfloat16)
    return (grad_tokens, grad_probs, grad_gate, grad_up, grad_down)


def solution(mesh):
    in_specs = (
        P(("dp", "expert"), None),
        P(("dp", "expert"), None),
        P(("dp", "expert"), None),
        P(("dp", "expert"), None),
        P(),
        P(),
        P("expert", "dp", None),
        P("expert", "dp", None),
        P("expert", None, "dp"),
    )
    out_specs = (
        P(("dp", "expert"), None),
        P(("dp", "expert"), None),
        P("expert", "dp", None),
        P("expert", "dp", None),
        P("expert", None, "dp"),
    )
    few = mesh.shape["expert"] <= 8 and mesh.shape["dp"] == 4
    body = gathered if few else shards
    return jax.shard_map(body, mesh=mesh, in_specs=in_specs, out_specs=out_specs, check_vma=False)
```

```python
import jax
import jax.numpy as jnp
from jax import lax
from jax.experimental import pallas as pl
from jax.experimental.pallas import tpu as pltpu
from jax.sharding import PartitionSpec as P

BF = jnp.bfloat16
F32 = jnp.float32


def contract(left, right, dim_left, dim_right):
    return lax.dot_general(
        left, right, (((dim_left,), (dim_right,)), ((), ())), preferred_element_type=F32
    )


def matchings(size):
    def pairs_of(left):
        if not left:
            yield []
            return
        for other in left[1:]:
            rest = [one for one in left[1:] if one != other]
            for tail in pairs_of(rest):
                yield [(left[0], other)] + tail

    tables = []
    for pairs in pairs_of(list(range(size))):
        table = [0] * size
        for a, b in pairs:
            table[a], table[b] = b, a
        tables.append(table)
    return tables


def dp_swap(value, bit):
    count = lax.axis_size("dp")
    return lax.ppermute(value, "dp", [(i, i ^ bit) for i in range(count)])


def core_swap(value):
    count = lax.axis_size("expert")
    return lax.ppermute(value, "expert", [(i, i ^ 1) for i in range(count)])


def chip_shift(value, step):
    count = lax.axis_size("expert")
    return lax.ppermute(value, "expert", [(i, (i + 2 * step) % count) for i in range(count)])


CHUNKS = (((1, 0), (3, 0)), ((2, 1), (3, 1)), ((0, 0), (2, 0)), ((0, 1), (1, 1)))
BLOCKS = tuple(key for chunk in CHUNKS for key in chunk)
LANES = 128
VMEM_LIMIT = 48 * 1024 * 1024
SMEM_SPEC = pl.BlockSpec(memory_space=pltpu.SMEM)
VMEM_SPEC = pl.BlockSpec(memory_space=pltpu.VMEM)
ANY_SPEC = pl.BlockSpec(memory_space=pltpu.HBM)


def shape_of(*dims, dtype=BF):
    return jax.ShapeDtypeStruct(dims, dtype)


def pack(place, holder, tokens, cotangent, probs, expert_ids, w_gate, w_up, w_down):
    rows, depth = tokens.shape
    span = holder.shape[0]
    tile, ff = w_gate.shape
    block = depth // 8
    picks = probs.shape[0]

    def kernel(place_ref, holder_ref, p_ref, id_ref, x_ref, dy_ref, g_ref, u_ref, d_ref, *rest):
        t_out, r_out, down_s, flip_s, share_s, sem_d, sem_w, sem_r, sem_o = rest
        here = place_ref[0]
        load_down = pltpu.make_async_copy(d_ref, down_s, sem_d)
        load_down.start()
        copies = []
        for at, source in enumerate((g_ref, u_ref)):
            copies.append(
                pltpu.make_async_copy(source, t_out.at[:, pl.ds(at * ff, ff)], sem_w.at[at])
            )
        for at, (quarter, half) in enumerate(BLOCKS):
            start = pl.multiple_of(((here ^ quarter) * 2 + half) * block, block)
            for which, source in enumerate((x_ref, dy_ref)):
                copies.append(
                    pltpu.make_async_copy(
                        source.at[:, pl.ds(start, block)],
                        r_out.at[:, pl.ds(which * depth + at * block, block)],
                        sem_r.at[2 * at + which],
                    )
                )
        start_all(copies)
        slots = lax.broadcasted_iota(jnp.int32, (LANES, rows), 0)
        share = jnp.zeros((LANES, rows), F32)
        for pick in range(picks):
            chosen = id_ref[pick : pick + 1, :]
            value = p_ref[pick : pick + 1, :].astype(F32)
            for slot in range(span):
                hit = (slots == slot) & (chosen == holder_ref[slot])
                share = jnp.where(hit, value, share)
        share_s[...] = share.T.astype(BF)
        load_down.wait()
        flip_s[...] = down_s[...].T
        late = [
            pltpu.make_async_copy(share_s, r_out.at[:, pl.ds(2 * depth, LANES)], sem_o.at[0]),
            pltpu.make_async_copy(flip_s, t_out.at[:, pl.ds(2 * ff, ff)], sem_o.at[1]),
        ]
        start_all(late)
        wait_all(copies)
        wait_all(late)

    return pl.pallas_call(
        kernel,
        out_shape=[
            shape_of(tile, 3 * ff),
            shape_of(rows, 2 * depth + LANES),
        ],
        in_specs=[SMEM_SPEC] * 2 + [VMEM_SPEC] * 2 + [ANY_SPEC] * 5,
        out_specs=[ANY_SPEC] * 2,
        scratch_shapes=[
            pltpu.VMEM((ff, tile), BF),
            pltpu.VMEM((tile, ff), BF),
            pltpu.VMEM((rows, LANES), BF),
            pltpu.SemaphoreType.DMA,
            pltpu.SemaphoreType.DMA((2,)),
            pltpu.SemaphoreType.DMA((16,)),
            pltpu.SemaphoreType.DMA((2,)),
        ],
        compiler_params=pltpu.CompilerParams(vmem_limit_bytes=VMEM_LIMIT),
        name="pack",
    )(place, holder, probs, expert_ids, tokens, cotangent, w_gate, w_up, w_down)


def gather_tiles(tile):
    half = tile.shape[0] // 2
    from_x = dp_swap(tile, 1)
    from_y = dp_swap(tile, 2)
    return tile, from_x, from_y, dp_swap(from_x[:half], 2), dp_swap(from_y[half:], 1)


def block_source(tiles, key, half):
    own, from_x, from_y, far_low, far_high = tiles
    quarter, side = key
    if quarter == 3:
        return (far_high if side else far_low), 0
    return (own, from_x, from_y)[quarter], side * half


def tile_copies(tiles, half, column, width, target, target_column, sems, base):
    copies = []
    for at, key in enumerate(BLOCKS):
        source, first = block_source(tiles, key, half)
        copies.append(
            pltpu.make_async_copy(
                source.at[pl.ds(first, half), pl.ds(column, width)],
                target.at[pl.ds(at * half, half), pl.ds(target_column, width)],
                sems.at[base + at],
            )
        )
    return copies


def gather_rows(block):
    chips = lax.axis_size("expert") // 2
    own = [block]
    for _ in range(chips - 1):
        own.append(chip_shift(own[-1], 1))
    return own + [core_swap(one) for one in own]


def start_all(copies):
    for copy in copies:
        copy.start()


def wait_all(copies):
    for copy in copies:
        copy.wait()


def weight_of(shares, index):
    lanes = lax.broadcasted_iota(jnp.int32, shares.shape, 1)
    return jnp.sum(jnp.where(lanes == index, shares.astype(F32), 0.0), axis=1, keepdims=True)


def row_copies(parts, column, width, target, sems):
    rows = parts[0].shape[0]
    return [
        pltpu.make_async_copy(
            part.at[:, pl.ds(column, width)], target.at[pl.ds(at * rows, rows)], sems.at[at]
        )
        for at, part in enumerate(parts)
    ]


def expert_pass(index, parts, tiles, depth, ff):
    count = len(parts)
    rows = parts[0].shape[0]
    total = count * rows
    half = tiles[0].shape[0] // 2
    group = 2 * rows
    n_tiles = len(tiles)
    n_in = 1 + count + n_tiles

    def kernel(*refs):
        index_ref = refs[0]
        part_refs = refs[1 : 1 + count]
        tile_refs = refs[1 + count : n_in]
        d_out, hw_out, score_out, near_out, away_out = refs[n_in : n_in + 5]
        x_s, dy_s, share_s, w_s, wd_s, d_s, hw_s, gt_s, sem_w, sem_d, sem_x, sem_s, sem_y, sem_o = (
            refs[n_in + 5 :]
        )
        w_copies = tile_copies(tile_refs, half, 0, 2 * ff, w_s, 0, sem_w, 0)
        x_copies = row_copies(part_refs, 0, depth, x_s, sem_x)
        s_copies = row_copies(part_refs, 2 * depth, LANES, share_s, sem_s)
        d_copies = tile_copies(tile_refs, half, 2 * ff, ff, wd_s, 0, sem_d, 0)
        y_copies = row_copies(part_refs, depth, depth, dy_s, sem_y)
        for copies in (w_copies, x_copies, s_copies, d_copies, y_copies):
            start_all(copies)
        for copies in (w_copies, x_copies, s_copies):
            wait_all(copies)

        def pre(place):
            both = jnp.dot(x_s[place, :], w_s[...], preferred_element_type=F32)
            weight = weight_of(share_s[place, :], index_ref[0])
            gate, up = both[:, :ff], both[:, ff:]
            sig = jax.nn.sigmoid(gate)
            act = gate * sig
            hid = (act * up).astype(BF).astype(F32)
            hw_s[place, :] = (hid * weight).astype(BF)
            return weight, act, hid, up * sig * (1.0 + gate * (1.0 - sig))

        def post(place, to, made):
            weight, act, hid, slope = made
            plain = jnp.dot(dy_s[place, :], wd_s[...], preferred_element_type=F32)
            score_out[place, :] = jnp.sum(hid * plain, axis=1, keepdims=True)
            d_hidden = plain * weight
            d_s[place, :ff] = (d_hidden * slope).astype(BF)
            d_s[place, ff:] = (d_hidden * act).astype(BF)
            gt_s[place, :] = contract(d_s[place, :], w_s[...], 1, 1).astype(BF)

        out_copies = []
        first = True
        for at in (2, 3, 0, 1):
            place = pl.ds(at * group, group)
            made = pre(place)
            if first:
                wait_all(d_copies)
                wait_all(y_copies)
                first = False
            post(place, None, made)
            target = away_out if at >= 2 else near_out
            out_copies.append(
                pltpu.make_async_copy(
                    gt_s.at[place], target.at[pl.ds(at % 2 * group, group)], sem_o.at[at]
                )
            )
            out_copies[-1].start()
            for which, (source, out) in enumerate(((d_s, d_out), (hw_s, hw_out))):
                out_copies.append(
                    pltpu.make_async_copy(
                        source.at[place], out.at[place], sem_o.at[4 + 4 * which + at]
                    )
                )
                out_copies[-1].start()
        wait_all(out_copies)

    return pl.pallas_call(
        kernel,
        out_shape=[
            shape_of(total, 2 * ff),
            shape_of(total, ff),
            shape_of(total, 1, dtype=F32),
            shape_of(total // 2, depth),
            shape_of(total // 2, depth),
        ],
        in_specs=[SMEM_SPEC] + [ANY_SPEC] * (count + n_tiles),
        out_specs=[ANY_SPEC, ANY_SPEC, VMEM_SPEC, ANY_SPEC, ANY_SPEC],
        scratch_shapes=[
            pltpu.VMEM((total, depth), BF),
            pltpu.VMEM((total, depth), BF),
            pltpu.VMEM((total, LANES), BF),
            pltpu.VMEM((depth, 2 * ff), BF),
            pltpu.VMEM((depth, ff), BF),
            pltpu.VMEM((total, 2 * ff), BF),
            pltpu.VMEM((total, ff), BF),
            pltpu.VMEM((total, depth), BF),
            pltpu.SemaphoreType.DMA((len(BLOCKS),)),
            pltpu.SemaphoreType.DMA((len(BLOCKS),)),
            pltpu.SemaphoreType.DMA((count,)),
            pltpu.SemaphoreType.DMA((count,)),
            pltpu.SemaphoreType.DMA((count,)),
            pltpu.SemaphoreType.DMA((12,)),
        ],
        compiler_params=pltpu.CompilerParams(vmem_limit_bytes=VMEM_LIMIT),
        name="expert_pass",
    )(index, *parts, *tiles)


def chunk_pair(parts, d_both, weighted, depth, first, name):
    count = len(parts)
    total = d_both.shape[0]
    ff = weighted.shape[1]
    width = depth // 4

    def kernel(*refs):
        part_refs = refs[:count]
        d_ref, hw_ref = refs[count : count + 2]
        outs = refs[count + 2 : count + 8]
        dy_s, x_s, hw_s, d_s, sem_y, sem_x, sem = refs[count + 8 :]
        load_hw = pltpu.make_async_copy(hw_ref, hw_s, sem.at[0])
        load_d = pltpu.make_async_copy(d_ref, d_s, sem.at[1])
        y_copies = row_copies(part_refs, depth + first * width, 2 * width, dy_s, sem_y)
        x_copies = row_copies(part_refs, first * width, 2 * width, x_s, sem_x)
        load_hw.start()
        start_all(y_copies)
        load_d.start()
        start_all(x_copies)
        load_hw.wait()
        wait_all(y_copies)
        for at in range(2):
            right = dy_s[:, at * width : (at + 1) * width]
            outs[at][...] = contract(hw_s[...], right, 0, 0).astype(BF)
        load_d.wait()
        wait_all(x_copies)
        for at in range(2):
            left = x_s[:, at * width : (at + 1) * width]
            outs[2 + at][...] = contract(left, d_s[:, :ff], 0, 0).astype(BF)
            outs[4 + at][...] = contract(left, d_s[:, ff:], 0, 0).astype(BF)

    return pl.pallas_call(
        kernel,
        out_shape=[shape_of(ff, width)] * 2 + [shape_of(width, ff)] * 4,
        in_specs=[ANY_SPEC] * (count + 2),
        out_specs=[VMEM_SPEC] * 6,
        scratch_shapes=[
            pltpu.VMEM((total, 2 * width), BF),
            pltpu.VMEM((total, 2 * width), BF),
            pltpu.VMEM((total, ff), BF),
            pltpu.VMEM((total, 2 * ff), BF),
            pltpu.SemaphoreType.DMA((count,)),
            pltpu.SemaphoreType.DMA((count,)),
            pltpu.SemaphoreType.DMA((2,)),
        ],
        compiler_params=pltpu.CompilerParams(vmem_limit_bytes=VMEM_LIMIT),
        name=name,
    )(*parts, d_both, weighted)


def unpack_rows(place, value):
    rows, depth = value.shape
    block = depth // 8

    def kernel(place_ref, v_ref, out_ref):
        here = place_ref[0]
        for at, (quarter, half) in enumerate(BLOCKS):
            start = pl.multiple_of(((here ^ quarter) * 2 + half) * block, block)
            out_ref[:, pl.ds(start, block)] = v_ref[:, at * block : (at + 1) * block]

    return pl.pallas_call(
        kernel,
        out_shape=shape_of(rows, depth),
        in_specs=[SMEM_SPEC, VMEM_SPEC],
        out_specs=VMEM_SPEC,
        compiler_params=pltpu.CompilerParams(vmem_limit_bytes=VMEM_LIMIT),
        name="unpack_rows",
    )(place, value)


def finish_reduce(got_x, got_y, keep_low, keep_high, axis):
    half = keep_low.shape[axis] // 2
    near = lambda v: lax.slice_in_dim(v, 0, half, axis=axis).astype(F32)
    far = lambda v: lax.slice_in_dim(v, half, 2 * half, axis=axis).astype(F32)
    pass_low = dp_swap((far(keep_low) + far(got_x)).astype(BF), 2)
    pass_high = dp_swap((far(keep_high) + far(got_y)).astype(BF), 1)
    low = near(keep_low) + near(got_x) + pass_low.astype(F32)
    high = near(keep_high) + near(got_y) + pass_high.astype(F32)
    return jnp.concatenate([low.astype(BF), high.astype(BF)], axis=axis)


def both_swaps(send_x, send_y):
    return lax.optimization_barrier((dp_swap(send_x, 1), dp_swap(send_y, 2)))


def gathered(tokens, cotangent, probs, expert_ids, holder, partner, w_gate, w_up, w_down):
    span = lax.axis_size("expert")
    chips = span // 2
    rows, depth = tokens.shape
    ff = w_gate.shape[2]
    place = lax.axis_index("dp")[None].astype(jnp.int32)
    index = lax.axis_index("expert").astype(jnp.int32)
    chip, core = index // 2, index % 2

    tile, packed = pack(
        place, holder, tokens, cotangent, probs.T, expert_ids.T, w_gate[0], w_up[0], w_down[0]
    )
    tiles = gather_tiles(tile)
    parts = gather_rows(packed)
    d_both, weighted, score, near, away = expert_pass(index[None], parts, tiles, depth, ff)
    got_rows = core_swap(away)
    sends = chunk_pair(parts, d_both, weighted, depth, 0, "sent_chunks")
    got = [both_swaps(sends[2 * w], sends[2 * w + 1]) for w in range(3)]
    both = (near.astype(F32) + got_rows.astype(F32)).astype(BF)
    late, _, _ = lax.optimization_barrier((weighted, sends[0], both))
    keeps = chunk_pair(parts, d_both, late, depth, 2, "kept_chunks")

    pieces = [both[s * rows : (s + 1) * rows] for s in range(chips)]
    total = pieces[-1]
    sums = []
    for w in range(3):
        if w < chips - 1:
            passed = chip_shift(total, -1).astype(F32)
            total = (pieces[chips - 2 - w].astype(F32) + passed).astype(BF)
        got_w, total = lax.optimization_barrier((got[w], total))
        sums.append(finish_reduce(*got_w, keeps[2 * w], keeps[2 * w + 1], 1 if w == 0 else 0))
    for s in range(chips - 5, -1, -1):
        total = (pieces[s].astype(F32) + chip_shift(total, -1).astype(F32)).astype(BF)
    down_sum, gate_sum, up_sum = sums
    grad_tokens = unpack_rows(place, total)

    everyone = jnp.arange(span, dtype=jnp.int32)
    steps = jnp.arange(chips, dtype=jnp.int32)
    own_chips = (chip - steps) % chips
    order = jnp.concatenate([2 * own_chips + core, 2 * own_chips + 1 - core])
    back = jnp.sum((order[None, :] == everyone[:, None]) * everyone[None, :], axis=1)
    by_device = jnp.take(score.reshape(span, rows), back, axis=0)
    got = lax.all_to_all(by_device, "expert", split_axis=0, concat_axis=0, tiled=True)
    hits = expert_ids[:, :, None] == holder[None, None, :]
    picked = jnp.sum(jnp.where(hits, got.T[:, None, :], 0.0), axis=2)
    grad_probs = picked.astype(BF)

    tables = matchings(span)
    chosen = jnp.argmax(jnp.all(jnp.array(tables, jnp.int32) == partner[None, :], axis=1))

    def trade(table):
        pairs = list(enumerate(table))
        return lambda *values: tuple(lax.ppermute(v, "expert", pairs) for v in values)

    branches = [trade(table) for table in tables]
    down_sum, gate_sum, total = lax.optimization_barrier((down_sum, gate_sum, total))
    grad_down, grad_gate = lax.switch(chosen, branches, down_sum, gate_sum)
    up_sum, grad_down, grad_gate = lax.optimization_barrier((up_sum, grad_down, grad_gate))
    (grad_up,) = lax.switch(chosen, branches, up_sum)
    return grad_tokens, grad_probs, grad_gate[None], grad_up[None], grad_down[None]


def contract_last(left, right):
    return lax.dot_general(
        left, right, (((1,), (1,)), ((), ())), preferred_element_type=jnp.float32
    )


def contract_first(left, right):
    return lax.dot_general(
        left, right, (((0,), (0,)), ((), ())), preferred_element_type=jnp.float32
    )


def move_weights(gate_tile, up_tile, down_tile, partner):
    spread = (
        lax.all_to_all(gate_tile, "expert", split_axis=1, concat_axis=0, tiled=True),
        lax.all_to_all(up_tile, "expert", split_axis=1, concat_axis=0, tiled=True),
        lax.all_to_all(down_tile, "expert", split_axis=1, concat_axis=0, tiled=True),
    )
    chosen = [jnp.take(piece, partner, axis=0) for piece in spread]
    return (
        lax.all_to_all(chosen[0], "expert", split_axis=0, concat_axis=1, tiled=True),
        lax.all_to_all(chosen[1], "expert", split_axis=0, concat_axis=1, tiled=True),
        lax.all_to_all(chosen[2], "expert", split_axis=0, concat_axis=1, tiled=True),
    )


def shards(tokens, cotangent, probs, expert_ids, holder, partner, w_gate, w_up, w_down):
    experts = holder.shape[0]
    span_size = lax.axis_size("expert")
    tok_rows, picks = expert_ids.shape
    pair_count = tok_rows * picks
    capacity = 2 * pair_count // experts
    numbers = jnp.arange(experts, dtype=jnp.int32)
    holder_hits = (holder[None, :] == numbers[:, None]).astype(jnp.int32)
    home_slot = jnp.sum(holder_hits * numbers[None, :], axis=1)
    gate_tile, up_tile, down_tile = move_weights(w_gate, w_up, w_down, partner)
    partner_hits = (home_slot[:, None] == numbers[None, :]).astype(jnp.int32)
    target = jnp.sum(partner_hits * partner[None, :], axis=1)
    full_gate, full_up, full_down = (
        lax.all_gather(gate_tile, "dp", axis=1, tiled=True),
        lax.all_gather(up_tile, "dp", axis=1, tiled=True),
        lax.all_gather(down_tile, "dp", axis=2, tiled=True),
    )
    gate_w = full_gate[0]
    up_w = full_up[0]
    down_w = full_down[0]
    flat_ids = expert_ids.reshape(pair_count)
    onehot = (flat_ids[:, None] == numbers[None, :]).astype(jnp.int32)
    earlier = jnp.cumsum(onehot, axis=0) - onehot
    slot_index = jnp.sum(earlier * onehot, axis=1)
    dest_dev = jnp.sum(onehot * target[None, :], axis=1)
    pair_row = dest_dev * capacity + slot_index
    row_table = (
        jnp.full((span_size * capacity,), pair_count, jnp.int32)
        .at[pair_row]
        .set(jnp.arange(pair_count, dtype=jnp.int32))
    )
    token_of_row = row_table // picks
    zero_row = jnp.zeros((1, tokens.shape[1]), jnp.bfloat16)
    send_x = jnp.concatenate([tokens, zero_row], axis=0)[token_of_row]
    send_dy = jnp.concatenate([cotangent, zero_row], axis=0)[token_of_row]
    send_p = jnp.concatenate([probs.reshape(pair_count), jnp.zeros((1,), jnp.bfloat16)], axis=0)[
        row_table
    ]
    send_scaled = (send_p.astype(jnp.float32)[:, None] * send_dy.astype(jnp.float32)).astype(
        jnp.bfloat16
    )
    recv_x, scaled = (
        lax.all_to_all(send_x, "expert", split_axis=0, concat_axis=0, tiled=True),
        lax.all_to_all(send_scaled, "expert", split_axis=0, concat_axis=0, tiled=True),
    )
    gate_pre = jnp.dot(recv_x, gate_w, preferred_element_type=jnp.float32)
    up_pre = jnp.dot(recv_x, up_w, preferred_element_type=jnp.float32)
    gate_sig = jax.nn.sigmoid(gate_pre)
    hidden = (gate_pre * gate_sig * up_pre).astype(jnp.bfloat16)
    expert_out = jnp.dot(hidden, down_w, preferred_element_type=jnp.float32).astype(jnp.bfloat16)
    d_hidden = contract_last(scaled, down_w)
    d_gate = (d_hidden * up_pre * gate_sig * (1.0 + gate_pre * (1.0 - gate_sig))).astype(
        jnp.bfloat16
    )
    d_up = (d_hidden * gate_pre * gate_sig).astype(jnp.bfloat16)
    pair_grad = (contract_last(d_gate, gate_w) + contract_last(d_up, up_w)).astype(jnp.bfloat16)
    back_out, back_grad = (
        lax.all_to_all(expert_out, "expert", split_axis=0, concat_axis=0, tiled=True),
        lax.all_to_all(pair_grad, "expert", split_axis=0, concat_axis=0, tiled=True),
    )
    row_score = jnp.sum(send_dy.astype(jnp.float32) * back_out.astype(jnp.float32), axis=1).astype(
        jnp.bfloat16
    )
    grad_probs = row_score[pair_row].reshape(tok_rows, picks)
    picked_rows = back_grad[pair_row].reshape(tok_rows, picks, back_grad.shape[1])
    grad_tokens = jnp.sum(picked_rows.astype(jnp.float32), axis=1).astype(jnp.bfloat16)
    shares = (
        lax.psum_scatter(
            contract_first(recv_x, d_gate)[None].astype(jnp.bfloat16),
            "dp",
            scatter_dimension=1,
            tiled=True,
        ).astype(jnp.float32),
        lax.psum_scatter(
            contract_first(recv_x, d_up)[None].astype(jnp.bfloat16),
            "dp",
            scatter_dimension=1,
            tiled=True,
        ).astype(jnp.float32),
        lax.psum_scatter(
            contract_first(hidden, scaled)[None].astype(jnp.bfloat16),
            "dp",
            scatter_dimension=2,
            tiled=True,
        ).astype(jnp.float32),
    )
    grad_gate = shares[0].astype(jnp.bfloat16)
    grad_up = shares[1].astype(jnp.bfloat16)
    grad_down = shares[2].astype(jnp.bfloat16)
    return (grad_tokens, grad_probs, grad_gate, grad_up, grad_down)


def solution(mesh):
    in_specs = (
        P(("dp", "expert"), None),
        P(("dp", "expert"), None),
        P(("dp", "expert"), None),
        P(("dp", "expert"), None),
        P(),
        P(),
        P("expert", "dp", None),
        P("expert", "dp", None),
        P("expert", None, "dp"),
    )
    out_specs = (
        P(("dp", "expert"), None),
        P(("dp", "expert"), None),
        P("expert", "dp", None),
        P("expert", "dp", None),
        P("expert", None, "dp"),
    )
    few = mesh.shape["expert"] <= 8 and mesh.shape["dp"] == 4
    body = gathered if few else shards
    return jax.shard_map(body, mesh=mesh, in_specs=in_specs, out_specs=out_specs, check_vma=False)
```

```python
import jax
import jax.numpy as jnp
from jax import lax
from jax.experimental import pallas as pl
from jax.experimental.pallas import tpu as pltpu
from jax.sharding import PartitionSpec as P

BF = jnp.bfloat16
F32 = jnp.float32


def contract(left, right, dim_left, dim_right):
    return lax.dot_general(
        left, right, (((dim_left,), (dim_right,)), ((), ())), preferred_element_type=F32
    )


def matchings(size):
    def pairs_of(left):
        if not left:
            yield []
            return
        for other in left[1:]:
            rest = [one for one in left[1:] if one != other]
            for tail in pairs_of(rest):
                yield [(left[0], other)] + tail

    tables = []
    for pairs in pairs_of(list(range(size))):
        table = [0] * size
        for a, b in pairs:
            table[a], table[b] = b, a
        tables.append(table)
    return tables


def dp_swap(value, bit):
    count = lax.axis_size("dp")
    return lax.ppermute(value, "dp", [(i, i ^ bit) for i in range(count)])


def core_swap(value):
    count = lax.axis_size("expert")
    return lax.ppermute(value, "expert", [(i, i ^ 1) for i in range(count)])


def chip_shift(value, step):
    count = lax.axis_size("expert")
    return lax.ppermute(value, "expert", [(i, (i + 2 * step) % count) for i in range(count)])


CHUNKS = (((1, 0), (3, 0)), ((2, 1), (3, 1)), ((0, 0), (2, 0)), ((0, 1), (1, 1)))
BLOCKS = tuple(key for chunk in CHUNKS for key in chunk)
LANES = 128
VMEM_LIMIT = 48 * 1024 * 1024
SMEM_SPEC = pl.BlockSpec(memory_space=pltpu.SMEM)
VMEM_SPEC = pl.BlockSpec(memory_space=pltpu.VMEM)
ANY_SPEC = pl.BlockSpec(memory_space=pltpu.HBM)


def shape_of(*dims, dtype=BF):
    return jax.ShapeDtypeStruct(dims, dtype)


def shares_of(ff):
    first = ff // 2
    return ((0, first), (first, ff - first))


def pack(place, holder, tokens, cotangent, probs, expert_ids, w_gate, w_up, w_down):
    rows, depth = tokens.shape
    span = holder.shape[0]
    tile, ff = w_gate.shape
    sides = shares_of(ff)
    block = depth // 8
    picks = probs.shape[0]

    def kernel(place_ref, holder_ref, p_ref, id_ref, x_ref, dy_ref, g_ref, u_ref, d_ref, *rest):
        t0_out, t1_out, r_out, down_s, sem_d, sem_w, sem_r = rest
        tiles = (t0_out, t1_out)
        here = place_ref[0]
        load_down = pltpu.make_async_copy(d_ref, down_s, sem_d)
        load_down.start()
        copies = []
        for side, (begin, part) in enumerate(sides):
            for at, source in enumerate((g_ref, u_ref)):
                copies.append(
                    pltpu.make_async_copy(
                        source.at[:, pl.ds(begin, part)],
                        tiles[side].at[:, pl.ds(at * part, part)],
                        sem_w.at[2 * side + at],
                    )
                )
        for at, (quarter, half) in enumerate(BLOCKS):
            start = pl.multiple_of(((here ^ quarter) * 2 + half) * block, block)
            for which, source in enumerate((x_ref, dy_ref)):
                copies.append(
                    pltpu.make_async_copy(
                        source.at[:, pl.ds(start, block)],
                        r_out.at[:, pl.ds(which * depth + at * block, block)],
                        sem_r.at[2 * at + which],
                    )
                )
        start_all(copies)
        slots = lax.broadcasted_iota(jnp.int32, (LANES, rows), 0)
        share = jnp.zeros((LANES, rows), F32)
        for pick in range(picks):
            chosen = id_ref[pick : pick + 1, :]
            value = p_ref[pick : pick + 1, :].astype(F32)
            for slot in range(span):
                hit = (slots == slot) & (chosen == holder_ref[slot])
                share = jnp.where(hit, value, share)
        r_out[:, 2 * depth :] = share.T.astype(BF)
        load_down.wait()
        for side, (begin, part) in enumerate(sides):
            tiles[side][:, 2 * part :] = down_s[begin : begin + part, :].T
        wait_all(copies)

    return pl.pallas_call(
        kernel,
        out_shape=[
            shape_of(tile, 3 * sides[0][1]),
            shape_of(tile, 3 * sides[1][1]),
            shape_of(rows, 2 * depth + LANES),
        ],
        in_specs=[SMEM_SPEC] * 2 + [VMEM_SPEC] * 2 + [ANY_SPEC] * 5,
        out_specs=[VMEM_SPEC] * 3,
        scratch_shapes=[
            pltpu.VMEM((ff, tile), BF),
            pltpu.SemaphoreType.DMA,
            pltpu.SemaphoreType.DMA((4,)),
            pltpu.SemaphoreType.DMA((16,)),
        ],
        compiler_params=pltpu.CompilerParams(vmem_limit_bytes=VMEM_LIMIT),
        name="pack",
    )(
        place,
        holder,
        probs,
        expert_ids,
        *(
            pltpu.with_memory_space_constraint(value, pltpu.HBM)
            for value in (tokens, cotangent, w_gate, w_up, w_down)
        ),
    )


def pass_tiles(from_x, from_y):
    half = from_x.shape[0] // 2
    return dp_swap(from_x[:half], 2), dp_swap(from_y[half:], 1)


def block_source(tiles, key, half):
    own, from_x, from_y, far_low, far_high = tiles
    quarter, side = key
    if quarter == 3:
        return (far_high if side else far_low), 0
    return (own, from_x, from_y)[quarter], side * half


def tile_copies(tiles, half, column, width, target, target_column, sems, base):
    copies = []
    for at, key in enumerate(BLOCKS):
        source, first = block_source(tiles, key, half)
        copies.append(
            pltpu.make_async_copy(
                source.at[pl.ds(first, half), pl.ds(column, width)],
                target.at[pl.ds(at * half, half), pl.ds(target_column, width)],
                sems.at[base + at],
            )
        )
    return copies


def gather_rows(block, first_hop):
    chips = lax.axis_size("expert") // 2
    own = [block, first_hop]
    for _ in range(chips - 2):
        own.append(chip_shift(own[-1], 1))
    return own + [core_swap(one) for one in own]


def start_all(copies):
    for copy in copies:
        copy.start()


def wait_all(copies):
    for copy in copies:
        copy.wait()


def weight_of(shares, index):
    lanes = lax.broadcasted_iota(jnp.int32, shares.shape, 1)
    return jnp.sum(jnp.where(lanes == index, shares.astype(F32), 0.0), axis=1, keepdims=True)


def row_copies(parts, column, width, target, sems):
    rows = parts[0].shape[0]
    return [
        pltpu.make_async_copy(
            part.at[:, pl.ds(column, width)], target.at[pl.ds(at * rows, rows)], sems.at[at]
        )
        for at, part in enumerate(parts)
    ]


def expert_pass(index, parts, tiles, depth, ff):
    count = len(parts)
    rows = parts[0].shape[0]
    total = count * rows
    half = tiles[0].shape[0] // 2
    sides = shares_of(ff)
    group = 2 * rows
    n_tiles = len(tiles)
    n_in = 1 + count + n_tiles

    def kernel(*refs):
        index_ref = refs[0]
        part_refs = refs[1 : 1 + count]
        tile_refs = refs[1 + count : n_in]
        d_out, hw_out, near_out, away_out = refs[n_in : n_in + 4]
        x_s, dy_s, share_s, w_s, wd_s, d_s, hw_s, gt_s, sem_w, sem_d, sem_x, sem_s, sem_y, sem_o = (
            refs[n_in + 4 :]
        )
        w_copies, d_copies = [], []
        for side, (begin, part) in enumerate(sides):
            own = tile_refs[5 * side : 5 * side + 5]
            w_copies += tile_copies(own, half, 0, 2 * part, w_s, 2 * begin, sem_w, 8 * side)
            d_copies += tile_copies(own, half, 2 * part, part, wd_s, begin, sem_d, 8 * side)
        x_copies = row_copies(part_refs, 0, depth, x_s, sem_x)
        s_copies = row_copies(part_refs, 2 * depth, LANES, share_s, sem_s)
        y_copies = row_copies(part_refs, depth, depth, dy_s, sem_y)
        for copies in (w_copies, x_copies, s_copies, d_copies, y_copies):
            start_all(copies)
        for copies in (w_copies, x_copies, s_copies):
            wait_all(copies)

        def pre(place):
            both = jnp.dot(x_s[place, :], w_s[...], preferred_element_type=F32)
            made = []
            for side, (begin, part) in enumerate(sides):
                base = 2 * begin
                weight = weight_of(share_s[place, :], index_ref[side])
                gate, up = both[:, base : base + part], both[:, base + part : base + 2 * part]
                sig = jax.nn.sigmoid(gate)
                act = gate * sig
                hid = (act * up).astype(BF).astype(F32)
                hw_s[place, begin : begin + part] = (hid * weight).astype(BF)
                made.append((weight, act, hid, up * sig * (1.0 + gate * (1.0 - sig))))
            return made

        def post(place, made):
            plain = jnp.dot(dy_s[place, :], wd_s[...], preferred_element_type=F32)
            lanes = lax.broadcasted_iota(jnp.int32, (group, LANES), 1)
            scores = jnp.zeros((group, LANES), F32)
            for side, (weight, act, hid, slope) in enumerate(made):
                begin, part = sides[side]
                base = 2 * begin
                mine = plain[:, begin : begin + part]
                score = jnp.sum(hid * mine, axis=1, keepdims=True)
                scores = jnp.where(lanes == index_ref[side], score, scores)
                d_hidden = mine * weight
                d_s[place, base : base + part] = (d_hidden * slope).astype(BF)
                d_s[place, base + part : base + 2 * part] = (d_hidden * act).astype(BF)
            gt_s[place, :depth] = contract(d_s[place, :], w_s[...], 1, 1).astype(BF)
            gt_s[place, depth:] = scores.astype(BF)

        out_copies = []
        first = True
        for at in (2, 3, 0, 1):
            place = pl.ds(at * group, group)
            made = pre(place)
            if first:
                wait_all(d_copies)
                wait_all(y_copies)
                first = False
            post(place, made)
            target = away_out if at >= 2 else near_out
            out_copies.append(
                pltpu.make_async_copy(
                    gt_s.at[place], target.at[pl.ds(at % 2 * group, group)], sem_o.at[at]
                )
            )
            out_copies[-1].start()
            for which, (source, out) in enumerate(((d_s, d_out), (hw_s, hw_out))):
                out_copies.append(
                    pltpu.make_async_copy(
                        source.at[place], out.at[place], sem_o.at[4 + 4 * which + at]
                    )
                )
                out_copies[-1].start()
        wait_all(out_copies)

    return pl.pallas_call(
        kernel,
        out_shape=[
            shape_of(total, 2 * ff),
            shape_of(total, ff),
            shape_of(total // 2, depth + LANES),
            shape_of(total // 2, depth + LANES),
        ],
        in_specs=[SMEM_SPEC] + [ANY_SPEC] * (count + n_tiles),
        out_specs=[ANY_SPEC] * 4,
        scratch_shapes=[
            pltpu.VMEM((total, depth), BF),
            pltpu.VMEM((total, depth), BF),
            pltpu.VMEM((total, LANES), BF),
            pltpu.VMEM((depth, 2 * ff), BF),
            pltpu.VMEM((depth, ff), BF),
            pltpu.VMEM((total, 2 * ff), BF),
            pltpu.VMEM((total, ff), BF),
            pltpu.VMEM((total, depth + LANES), BF),
            pltpu.SemaphoreType.DMA((2 * len(BLOCKS),)),
            pltpu.SemaphoreType.DMA((2 * len(BLOCKS),)),
            pltpu.SemaphoreType.DMA((count,)),
            pltpu.SemaphoreType.DMA((count,)),
            pltpu.SemaphoreType.DMA((count,)),
            pltpu.SemaphoreType.DMA((12,)),
        ],
        compiler_params=pltpu.CompilerParams(vmem_limit_bytes=VMEM_LIMIT),
        name="expert_pass",
    )(index, *parts, *tiles)


def chunk_pair(parts, d_both, weighted, depth, first, name):
    count = len(parts)
    total = d_both.shape[0]
    ff = weighted.shape[1]
    width = depth // 4
    sides = shares_of(ff)

    def kernel(*refs):
        part_refs = refs[:count]
        d_ref, hw_ref = refs[count : count + 2]
        outs = refs[count + 2 : count + 6]
        dy_s, x_s, hw_s, d_s, sem_y, sem_x, sem = refs[count + 6 :]
        load_hw = pltpu.make_async_copy(hw_ref, hw_s, sem.at[0])
        load_d = pltpu.make_async_copy(d_ref, d_s, sem.at[1])
        y_copies = row_copies(part_refs, depth + first * width, 2 * width, dy_s, sem_y)
        x_copies = row_copies(part_refs, first * width, 2 * width, x_s, sem_x)
        load_d.start()
        start_all(x_copies)
        load_hw.start()
        start_all(y_copies)
        load_d.wait()
        wait_all(x_copies)
        load_hw.wait()
        wait_all(y_copies)
        for side, (begin, part) in enumerate(sides):
            for at in range(2):
                of = slice(at * width, (at + 1) * width)
                out = outs[2 * side + at]
                mine = d_s[:, 2 * begin : 2 * begin + 2 * part]
                out[:, : 2 * part] = contract(x_s[:, of], mine, 0, 0).astype(BF)
                mine = hw_s[:, begin : begin + part]
                out[:, 2 * part :] = contract(dy_s[:, of], mine, 0, 0).astype(BF)

    return pl.pallas_call(
        kernel,
        out_shape=[shape_of(width, 3 * part) for _, part in sides for _ in range(2)],
        in_specs=[ANY_SPEC] * (count + 2),
        out_specs=[VMEM_SPEC] * 4,
        scratch_shapes=[
            pltpu.VMEM((total, 2 * width), BF),
            pltpu.VMEM((total, 2 * width), BF),
            pltpu.VMEM((total, ff), BF),
            pltpu.VMEM((total, 2 * ff), BF),
            pltpu.SemaphoreType.DMA((count,)),
            pltpu.SemaphoreType.DMA((count,)),
            pltpu.SemaphoreType.DMA((2,)),
        ],
        compiler_params=pltpu.CompilerParams(vmem_limit_bytes=VMEM_LIMIT),
        name=name,
    )(*parts, d_both, weighted)


def unpack_weights(traded, stays, passed, ff):
    sides = shares_of(ff)
    rows = traded[0].shape[0]
    (_, one), (begin, two) = sides

    def kernel(*refs):
        traded_refs, stay_refs, passed_refs = refs[0:2], refs[2:4], refs[4:6]
        gate_out, up_out, down_out = refs[6:9]
        for at in range(2):
            of = slice(at * rows, (at + 1) * rows)
            first = traded_refs[at]
            other = (stay_refs[at][...] + passed_refs[at][...].astype(F32)).astype(BF)
            gate_out[of, :one] = first[:, :one]
            gate_out[of, begin:] = other[:, :two]
            up_out[of, :one] = first[:, one : 2 * one]
            up_out[of, begin:] = other[:, two : 2 * two]
            down_out[:one, of] = first[:, 2 * one :].T
            down_out[begin:, of] = other[:, 2 * two :].T

    return pl.pallas_call(
        kernel,
        out_shape=[shape_of(2 * rows, ff), shape_of(2 * rows, ff), shape_of(ff, 2 * rows)],
        in_specs=[VMEM_SPEC] * 6,
        out_specs=[VMEM_SPEC] * 3,
        compiler_params=pltpu.CompilerParams(vmem_limit_bytes=VMEM_LIMIT),
        name="unpack_weights",
    )(*traded, *stays, *passed)


def unpack_rows(place, value):
    rows = value.shape[0]
    depth = value.shape[1] - LANES
    block = depth // 8

    def kernel(place_ref, v_ref, out_ref):
        here = place_ref[0]
        for at, (quarter, half) in enumerate(BLOCKS):
            start = pl.multiple_of(((here ^ quarter) * 2 + half) * block, block)
            out_ref[:, pl.ds(start, block)] = v_ref[:, at * block : (at + 1) * block]

    return pl.pallas_call(
        kernel,
        out_shape=shape_of(rows, depth),
        in_specs=[SMEM_SPEC, VMEM_SPEC],
        out_specs=VMEM_SPEC,
        compiler_params=pltpu.CompilerParams(vmem_limit_bytes=VMEM_LIMIT),
        name="unpack_rows",
    )(place, value)


def summed(got, kept):
    half = got.shape[0] // 2
    stay = kept[:half].astype(F32) + got[:half].astype(F32)
    return stay, (kept[half:].astype(F32) + got[half:].astype(F32)).astype(BF)


def both_swaps(send_x, send_y):
    return lax.optimization_barrier((dp_swap(send_x, 1), dp_swap(send_y, 2)))


def gathered(tokens, cotangent, probs, expert_ids, holder, partner, w_gate, w_up, w_down):
    span = lax.axis_size("expert")
    chips = span // 2
    rows, depth = tokens.shape
    ff = w_gate.shape[2]
    place = lax.axis_index("dp")[None].astype(jnp.int32)
    index = lax.axis_index("expert").astype(jnp.int32)
    everyone = jnp.arange(span, dtype=jnp.int32)
    mate = jnp.sum(jnp.where(everyone == index, partner, 0))
    pair = jnp.stack([index, mate])
    tables = matchings(span)
    chosen = jnp.argmax(jnp.all(jnp.array(tables, jnp.int32) == partner[None, :], axis=1))

    def trade(table):
        pairs = list(enumerate(table))
        return lambda *values: tuple(lax.ppermute(v, "expert", pairs) for v in values)

    branches = [trade(table) for table in tables]

    tile_a, tile_b, packed = pack(
        place, holder, tokens, cotangent, probs.T, expert_ids.T, w_gate[0], w_up[0], w_down[0]
    )
    near_a = dp_swap(tile_a, 1), dp_swap(tile_a, 2)
    first_hop = chip_shift(packed, 1)
    (tile_b,) = lax.switch(chosen, branches, tile_b)
    tile_b, near_a, first_hop = lax.optimization_barrier((tile_b, near_a, first_hop))
    tile_b, far_a = lax.optimization_barrier((tile_b, pass_tiles(*near_a)))
    near_b = dp_swap(tile_b, 1), dp_swap(tile_b, 2)
    tiles = (tile_a,) + near_a + far_a + (tile_b,) + near_b + pass_tiles(*near_b)
    parts = gather_rows(packed, first_hop)
    d_both, weighted, near, away = expert_pass(pair, parts, tiles, depth, ff)
    got_rows = core_swap(away)
    sends = chunk_pair(parts, d_both, weighted, depth, 0, "sent_chunks")
    got_a = both_swaps(*sends[:2])
    near, _ = lax.optimization_barrier((near, sends[0]))
    both = (near.astype(F32) + got_rows.astype(F32)).astype(BF)
    pieces = [both[s * rows : (s + 1) * rows] for s in range(chips)]
    total = pieces[-1]

    def ring_step(total, s):
        return (pieces[s].astype(F32) + chip_shift(total, -1).astype(F32)).astype(BF)

    left = list(range(chips - 2, -1, -1))
    total = ring_step(total, left.pop(0))
    late, _, total = lax.optimization_barrier((weighted, sends[0], total))
    keeps = chunk_pair(parts, d_both, late, depth, 2, "kept_chunks")
    keeps, total = lax.optimization_barrier((keeps, total))
    if left:
        total = ring_step(total, left.pop(0))
    got_a, total = lax.optimization_barrier((got_a, total))
    stay_low, pass_low = summed(got_a[0], keeps[0])
    stay_high, pass_high = summed(got_a[1], keeps[1])
    passed = dp_swap(pass_low, 2), dp_swap(pass_high, 1)
    for s in left:
        total = ring_step(total, s)
    passed, sends_b = lax.optimization_barrier((passed, sends[2:]))
    got_b = both_swaps(*sends_b)
    low = (stay_low + passed[0].astype(F32)).astype(BF)
    high = (stay_high + passed[1].astype(F32)).astype(BF)
    low, high, total = lax.optimization_barrier((low, high, total))
    traded = lax.switch(chosen, branches, low, high)
    traded, got_b = lax.optimization_barrier((traded, got_b))
    stay_low, pass_low = summed(got_b[0], keeps[2])
    stay_high, pass_high = summed(got_b[1], keeps[3])
    passed = dp_swap(pass_low, 2), dp_swap(pass_high, 1)
    grad_gate, grad_up, grad_down = unpack_weights(traded, (stay_low, stay_high), passed, ff)

    grad_tokens = unpack_rows(place, total)
    by_slot = total[:, depth : depth + span].astype(F32)
    hits = expert_ids[:, :, None] == holder[None, None, :]
    grad_probs = jnp.sum(jnp.where(hits, by_slot[:, None, :], 0.0), axis=2).astype(BF)
    return grad_tokens, grad_probs, grad_gate[None], grad_up[None], grad_down[None]


def contract_last(left, right):
    return lax.dot_general(
        left, right, (((1,), (1,)), ((), ())), preferred_element_type=jnp.float32
    )


def contract_first(left, right):
    return lax.dot_general(
        left, right, (((0,), (0,)), ((), ())), preferred_element_type=jnp.float32
    )


def move_weights(gate_tile, up_tile, down_tile, partner):
    spread = (
        lax.all_to_all(gate_tile, "expert", split_axis=1, concat_axis=0, tiled=True),
        lax.all_to_all(up_tile, "expert", split_axis=1, concat_axis=0, tiled=True),
        lax.all_to_all(down_tile, "expert", split_axis=1, concat_axis=0, tiled=True),
    )
    chosen = [jnp.take(piece, partner, axis=0) for piece in spread]
    return (
        lax.all_to_all(chosen[0], "expert", split_axis=0, concat_axis=1, tiled=True),
        lax.all_to_all(chosen[1], "expert", split_axis=0, concat_axis=1, tiled=True),
        lax.all_to_all(chosen[2], "expert", split_axis=0, concat_axis=1, tiled=True),
    )


def shards(tokens, cotangent, probs, expert_ids, holder, partner, w_gate, w_up, w_down):
    experts = holder.shape[0]
    span_size = lax.axis_size("expert")
    tok_rows, picks = expert_ids.shape
    pair_count = tok_rows * picks
    capacity = 2 * pair_count // experts
    numbers = jnp.arange(experts, dtype=jnp.int32)
    holder_hits = (holder[None, :] == numbers[:, None]).astype(jnp.int32)
    home_slot = jnp.sum(holder_hits * numbers[None, :], axis=1)
    gate_tile, up_tile, down_tile = move_weights(w_gate, w_up, w_down, partner)
    partner_hits = (home_slot[:, None] == numbers[None, :]).astype(jnp.int32)
    target = jnp.sum(partner_hits * partner[None, :], axis=1)
    full_gate, full_up, full_down = (
        lax.all_gather(gate_tile, "dp", axis=1, tiled=True),
        lax.all_gather(up_tile, "dp", axis=1, tiled=True),
        lax.all_gather(down_tile, "dp", axis=2, tiled=True),
    )
    gate_w = full_gate[0]
    up_w = full_up[0]
    down_w = full_down[0]
    flat_ids = expert_ids.reshape(pair_count)
    onehot = (flat_ids[:, None] == numbers[None, :]).astype(jnp.int32)
    earlier = jnp.cumsum(onehot, axis=0) - onehot
    slot_index = jnp.sum(earlier * onehot, axis=1)
    dest_dev = jnp.sum(onehot * target[None, :], axis=1)
    pair_row = dest_dev * capacity + slot_index
    row_table = (
        jnp.full((span_size * capacity,), pair_count, jnp.int32)
        .at[pair_row]
        .set(jnp.arange(pair_count, dtype=jnp.int32))
    )
    token_of_row = row_table // picks
    zero_row = jnp.zeros((1, tokens.shape[1]), jnp.bfloat16)
    send_x = jnp.concatenate([tokens, zero_row], axis=0)[token_of_row]
    send_dy = jnp.concatenate([cotangent, zero_row], axis=0)[token_of_row]
    send_p = jnp.concatenate([probs.reshape(pair_count), jnp.zeros((1,), jnp.bfloat16)], axis=0)[
        row_table
    ]
    send_scaled = (send_p.astype(jnp.float32)[:, None] * send_dy.astype(jnp.float32)).astype(
        jnp.bfloat16
    )
    recv_x, scaled = (
        lax.all_to_all(send_x, "expert", split_axis=0, concat_axis=0, tiled=True),
        lax.all_to_all(send_scaled, "expert", split_axis=0, concat_axis=0, tiled=True),
    )
    gate_pre = jnp.dot(recv_x, gate_w, preferred_element_type=jnp.float32)
    up_pre = jnp.dot(recv_x, up_w, preferred_element_type=jnp.float32)
    gate_sig = jax.nn.sigmoid(gate_pre)
    hidden = (gate_pre * gate_sig * up_pre).astype(jnp.bfloat16)
    expert_out = jnp.dot(hidden, down_w, preferred_element_type=jnp.float32).astype(jnp.bfloat16)
    d_hidden = contract_last(scaled, down_w)
    d_gate = (d_hidden * up_pre * gate_sig * (1.0 + gate_pre * (1.0 - gate_sig))).astype(
        jnp.bfloat16
    )
    d_up = (d_hidden * gate_pre * gate_sig).astype(jnp.bfloat16)
    pair_grad = (contract_last(d_gate, gate_w) + contract_last(d_up, up_w)).astype(jnp.bfloat16)
    back_out, back_grad = (
        lax.all_to_all(expert_out, "expert", split_axis=0, concat_axis=0, tiled=True),
        lax.all_to_all(pair_grad, "expert", split_axis=0, concat_axis=0, tiled=True),
    )
    row_score = jnp.sum(send_dy.astype(jnp.float32) * back_out.astype(jnp.float32), axis=1).astype(
        jnp.bfloat16
    )
    grad_probs = row_score[pair_row].reshape(tok_rows, picks)
    picked_rows = back_grad[pair_row].reshape(tok_rows, picks, back_grad.shape[1])
    grad_tokens = jnp.sum(picked_rows.astype(jnp.float32), axis=1).astype(jnp.bfloat16)
    shares = (
        lax.psum_scatter(
            contract_first(recv_x, d_gate)[None].astype(jnp.bfloat16),
            "dp",
            scatter_dimension=1,
            tiled=True,
        ).astype(jnp.float32),
        lax.psum_scatter(
            contract_first(recv_x, d_up)[None].astype(jnp.bfloat16),
            "dp",
            scatter_dimension=1,
            tiled=True,
        ).astype(jnp.float32),
        lax.psum_scatter(
            contract_first(hidden, scaled)[None].astype(jnp.bfloat16),
            "dp",
            scatter_dimension=2,
            tiled=True,
        ).astype(jnp.float32),
    )
    grad_gate = shares[0].astype(jnp.bfloat16)
    grad_up = shares[1].astype(jnp.bfloat16)
    grad_down = shares[2].astype(jnp.bfloat16)
    return (grad_tokens, grad_probs, grad_gate, grad_up, grad_down)


def solution(mesh):
    in_specs = (
        P(("dp", "expert"), None),
        P(("dp", "expert"), None),
        P(("dp", "expert"), None),
        P(("dp", "expert"), None),
        P(),
        P(),
        P("expert", "dp", None),
        P("expert", "dp", None),
        P("expert", None, "dp"),
    )
    out_specs = (
        P(("dp", "expert"), None),
        P(("dp", "expert"), None),
        P("expert", "dp", None),
        P("expert", "dp", None),
        P("expert", None, "dp"),
    )
    few = mesh.shape["expert"] <= 8 and mesh.shape["dp"] == 4
    body = gathered if few else shards
    return jax.shard_map(body, mesh=mesh, in_specs=in_specs, out_specs=out_specs, check_vma=False)
```

```python
import jax
import jax.numpy as jnp
from jax import lax
from jax.experimental import pallas as pl
from jax.experimental.pallas import tpu as pltpu
from jax.sharding import PartitionSpec as P

BF = jnp.bfloat16
F32 = jnp.float32


def contract(left, right, dim_left, dim_right):
    return lax.dot_general(
        left, right, (((dim_left,), (dim_right,)), ((), ())), preferred_element_type=F32
    )


def matchings(size):
    def pairs_of(left):
        if not left:
            yield []
            return
        for other in left[1:]:
            rest = [one for one in left[1:] if one != other]
            for tail in pairs_of(rest):
                yield [(left[0], other)] + tail

    tables = []
    for pairs in pairs_of(list(range(size))):
        table = [0] * size
        for a, b in pairs:
            table[a], table[b] = b, a
        tables.append(table)
    return tables


def dp_swap(value, bit):
    count = lax.axis_size("dp")
    return lax.ppermute(value, "dp", [(i, i ^ bit) for i in range(count)])


def core_swap(value):
    count = lax.axis_size("expert")
    return lax.ppermute(value, "expert", [(i, i ^ 1) for i in range(count)])


def chip_shift(value, step):
    count = lax.axis_size("expert")
    return lax.ppermute(value, "expert", [(i, (i + 2 * step) % count) for i in range(count)])


CHUNKS = (((1, 0), (3, 0)), ((2, 1), (3, 1)), ((0, 0), (2, 0)), ((0, 1), (1, 1)))
BLOCKS = tuple(key for chunk in CHUNKS for key in chunk)
LANES = 128
VMEM_LIMIT = 48 * 1024 * 1024
SMEM_SPEC = pl.BlockSpec(memory_space=pltpu.SMEM)
VMEM_SPEC = pl.BlockSpec(memory_space=pltpu.VMEM)
ANY_SPEC = pl.BlockSpec(memory_space=pltpu.HBM)


def shape_of(*dims, dtype=BF):
    return jax.ShapeDtypeStruct(dims, dtype)


def shares_of(ff):
    first = ff // 2
    return ((0, first), (first, ff - first))


def pack(place, holder, tokens, cotangent, probs, expert_ids, w_gate, w_up, w_down):
    rows, depth = tokens.shape
    span = holder.shape[0]
    tile, ff = w_gate.shape
    sides = shares_of(ff)
    block = depth // 8
    picks = probs.shape[0]

    def kernel(place_ref, holder_ref, p_ref, id_ref, x_ref, dy_ref, g_ref, u_ref, d_ref, *rest):
        t0_out, t1_out, r_out, down_s, sem_d, sem_w, sem_r = rest
        tiles = (t0_out, t1_out)
        here = place_ref[0]
        load_down = pltpu.make_async_copy(d_ref, down_s, sem_d)
        load_down.start()
        copies = []
        for side, (begin, part) in enumerate(sides):
            for at, source in enumerate((g_ref, u_ref)):
                copies.append(
                    pltpu.make_async_copy(
                        source.at[:, pl.ds(begin, part)],
                        tiles[side].at[:, pl.ds(at * part, part)],
                        sem_w.at[2 * side + at],
                    )
                )
        for at, (quarter, half) in enumerate(BLOCKS):
            start = pl.multiple_of(((here ^ quarter) * 2 + half) * block, block)
            for which, source in enumerate((x_ref, dy_ref)):
                copies.append(
                    pltpu.make_async_copy(
                        source.at[:, pl.ds(start, block)],
                        r_out.at[:, pl.ds(which * depth + at * block, block)],
                        sem_r.at[2 * at + which],
                    )
                )
        start_all(copies)
        slots = lax.broadcasted_iota(jnp.int32, (LANES, rows), 0)
        share = jnp.zeros((LANES, rows), F32)
        for pick in range(picks):
            chosen = id_ref[pick : pick + 1, :]
            value = p_ref[pick : pick + 1, :].astype(F32)
            for slot in range(span):
                hit = (slots == slot) & (chosen == holder_ref[slot])
                share = jnp.where(hit, value, share)
        r_out[:, 2 * depth :] = share.T.astype(BF)
        load_down.wait()
        for side, (begin, part) in enumerate(sides):
            tiles[side][:, 2 * part :] = down_s[begin : begin + part, :].T
        wait_all(copies)

    return pl.pallas_call(
        kernel,
        out_shape=[
            shape_of(tile, 3 * sides[0][1]),
            shape_of(tile, 3 * sides[1][1]),
            shape_of(rows, 2 * depth + LANES),
        ],
        in_specs=[SMEM_SPEC] * 2 + [VMEM_SPEC] * 2 + [ANY_SPEC] * 5,
        out_specs=[VMEM_SPEC] * 3,
        scratch_shapes=[
            pltpu.VMEM((ff, tile), BF),
            pltpu.SemaphoreType.DMA,
            pltpu.SemaphoreType.DMA((4,)),
            pltpu.SemaphoreType.DMA((16,)),
        ],
        compiler_params=pltpu.CompilerParams(vmem_limit_bytes=VMEM_LIMIT),
        name="pack",
    )(
        place,
        holder,
        probs,
        expert_ids,
        *(
            pltpu.with_memory_space_constraint(value, pltpu.HBM)
            for value in (tokens, cotangent, w_gate, w_up, w_down)
        ),
    )


def pass_tiles(from_x, from_y):
    half = from_x.shape[0] // 2
    return dp_swap(from_x[:half], 2), dp_swap(from_y[half:], 1)


def block_source(tiles, key, half):
    own, from_x, from_y, far_low, far_high = tiles
    quarter, side = key
    if quarter == 3:
        return (far_high if side else far_low), 0
    return (own, from_x, from_y)[quarter], side * half


def tile_copies(tiles, half, column, width, target, target_column, sems, base):
    copies = []
    for at, key in enumerate(BLOCKS):
        source, first = block_source(tiles, key, half)
        copies.append(
            pltpu.make_async_copy(
                source.at[pl.ds(first, half), pl.ds(column, width)],
                target.at[pl.ds(at * half, half), pl.ds(target_column, width)],
                sems.at[base + at],
            )
        )
    return copies


def start_all(copies):
    for copy in copies:
        copy.start()


def wait_all(copies):
    for copy in copies:
        copy.wait()


def weight_of(shares, index):
    lanes = lax.broadcasted_iota(jnp.int32, shares.shape, 1)
    return jnp.sum(jnp.where(lanes == index, shares.astype(F32), 0.0), axis=1, keepdims=True)


def row_copies(parts, column, width, target, sems):
    rows = parts[0].shape[0]
    return [
        pltpu.make_async_copy(
            part.at[:, pl.ds(column, width)], target.at[pl.ds(at * rows, rows)], sems.at[at]
        )
        for at, part in enumerate(parts)
    ]


def expert_pass(index, parts, tiles, depth, ff):
    count = len(parts)
    rows = parts[0].shape[0]
    total = count * rows
    half = tiles[0].shape[0] // 2
    sides = shares_of(ff)
    group = 2 * rows
    n_tiles = len(tiles)
    n_in = 1 + count + n_tiles

    def kernel(*refs):
        index_ref = refs[0]
        part_refs = refs[1 : 1 + count]
        tile_refs = refs[1 + count : n_in]
        d_out, hw_out, near_out, away_out = refs[n_in : n_in + 4]
        x_s, dy_s, share_s, w_s, wd_s, d_s, hw_s, gt_s, sem_w, sem_d, sem_x, sem_s, sem_y, sem_o = (
            refs[n_in + 4 :]
        )
        w_copies, d_copies = [], []
        for side, (begin, part) in enumerate(sides):
            own = tile_refs[5 * side : 5 * side + 5]
            w_copies += tile_copies(own, half, 0, 2 * part, w_s, 2 * begin, sem_w, 8 * side)
            d_copies += tile_copies(own, half, 2 * part, part, wd_s, begin, sem_d, 8 * side)
        x_copies = row_copies(part_refs, 0, depth, x_s, sem_x)
        s_copies = row_copies(part_refs, 2 * depth, LANES, share_s, sem_s)
        y_copies = row_copies(part_refs, depth, depth, dy_s, sem_y)
        for copies in (w_copies, x_copies, s_copies, d_copies, y_copies):
            start_all(copies)
        for copies in (w_copies, x_copies, s_copies):
            wait_all(copies)

        def pre(place):
            both = jnp.dot(x_s[place, :], w_s[...], preferred_element_type=F32)
            made = []
            for side, (begin, part) in enumerate(sides):
                base = 2 * begin
                weight = weight_of(share_s[place, :], index_ref[side])
                gate, up = both[:, base : base + part], both[:, base + part : base + 2 * part]
                sig = jax.nn.sigmoid(gate)
                act = gate * sig
                hid = (act * up).astype(BF).astype(F32)
                hw_s[place, begin : begin + part] = (hid * weight).astype(BF)
                made.append((weight, act, hid, up * sig * (1.0 + gate * (1.0 - sig))))
            return made

        def post(place, made):
            plain = jnp.dot(dy_s[place, :], wd_s[...], preferred_element_type=F32)
            lanes = lax.broadcasted_iota(jnp.int32, (group, LANES), 1)
            scores = jnp.zeros((group, LANES), F32)
            for side, (weight, act, hid, slope) in enumerate(made):
                begin, part = sides[side]
                base = 2 * begin
                mine = plain[:, begin : begin + part]
                score = jnp.sum(hid * mine, axis=1, keepdims=True)
                scores = jnp.where(lanes == index_ref[side], score, scores)
                d_hidden = mine * weight
                d_s[place, base : base + part] = (d_hidden * slope).astype(BF)
                d_s[place, base + part : base + 2 * part] = (d_hidden * act).astype(BF)
            gt_s[place, :depth] = contract(d_s[place, :], w_s[...], 1, 1).astype(BF)
            gt_s[place, depth:] = scores.astype(BF)

        out_copies = []
        first = True
        for at in (2, 3, 0, 1):
            place = pl.ds(at * group, group)
            made = pre(place)
            if first:
                wait_all(d_copies)
                wait_all(y_copies)
                first = False
            post(place, made)
            target = away_out if at >= 2 else near_out
            out_copies.append(
                pltpu.make_async_copy(
                    gt_s.at[place], target.at[pl.ds(at % 2 * group, group)], sem_o.at[at]
                )
            )
            out_copies[-1].start()
            for which, (source, out) in enumerate(((d_s, d_out), (hw_s, hw_out))):
                out_copies.append(
                    pltpu.make_async_copy(
                        source.at[place], out.at[place], sem_o.at[4 + 4 * which + at]
                    )
                )
                out_copies[-1].start()
        wait_all(out_copies)

    return pl.pallas_call(
        kernel,
        out_shape=[
            shape_of(total, 2 * ff),
            shape_of(total, ff),
            shape_of(total // 2, depth + LANES),
            shape_of(total // 2, depth + LANES),
        ],
        in_specs=[SMEM_SPEC] + [ANY_SPEC] * (count + n_tiles),
        out_specs=[ANY_SPEC] * 4,
        scratch_shapes=[
            pltpu.VMEM((total, depth), BF),
            pltpu.VMEM((total, depth), BF),
            pltpu.VMEM((total, LANES), BF),
            pltpu.VMEM((depth, 2 * ff), BF),
            pltpu.VMEM((depth, ff), BF),
            pltpu.VMEM((total, 2 * ff), BF),
            pltpu.VMEM((total, ff), BF),
            pltpu.VMEM((total, depth + LANES), BF),
            pltpu.SemaphoreType.DMA((2 * len(BLOCKS),)),
            pltpu.SemaphoreType.DMA((2 * len(BLOCKS),)),
            pltpu.SemaphoreType.DMA((count,)),
            pltpu.SemaphoreType.DMA((count,)),
            pltpu.SemaphoreType.DMA((count,)),
            pltpu.SemaphoreType.DMA((12,)),
        ],
        compiler_params=pltpu.CompilerParams(vmem_limit_bytes=VMEM_LIMIT),
        name="expert_pass",
    )(index, *parts, *tiles)


def chunks_of(parts, d_both, weighted, depth, first, number, side, name):
    count = len(parts)
    total = d_both.shape[0]
    ff = weighted.shape[1]
    width = depth // 4
    begin, part = shares_of(ff)[side]

    def kernel(*refs):
        part_refs = refs[:count]
        d_ref, hw_ref = refs[count : count + 2]
        outs = refs[count + 2 : count + 2 + number]
        dy_s, x_s, hw_s, d_s, sem_y, sem_x, sem = refs[count + 2 + number :]
        load_hw = pltpu.make_async_copy(hw_ref.at[:, pl.ds(begin, part)], hw_s, sem.at[0])
        load_d = pltpu.make_async_copy(d_ref.at[:, pl.ds(2 * begin, 2 * part)], d_s, sem.at[1])
        y_copies = row_copies(part_refs, depth + first * width, number * width, dy_s, sem_y)
        x_copies = row_copies(part_refs, first * width, number * width, x_s, sem_x)
        load_d.start()
        start_all(x_copies)
        load_hw.start()
        start_all(y_copies)
        load_d.wait()
        wait_all(x_copies)
        for at in range(number):
            of = slice(at * width, (at + 1) * width)
            outs[at][:, : 2 * part] = contract(x_s[:, of], d_s[...], 0, 0).astype(BF)
        load_hw.wait()
        wait_all(y_copies)
        for at in range(number):
            of = slice(at * width, (at + 1) * width)
            outs[at][:, 2 * part :] = contract(dy_s[:, of], hw_s[...], 0, 0).astype(BF)

    return pl.pallas_call(
        kernel,
        out_shape=[shape_of(width, 3 * part)] * number,
        in_specs=[ANY_SPEC] * (count + 2),
        out_specs=[VMEM_SPEC] * number,
        scratch_shapes=[
            pltpu.VMEM((total, number * width), BF),
            pltpu.VMEM((total, number * width), BF),
            pltpu.VMEM((total, part), BF),
            pltpu.VMEM((total, 2 * part), BF),
            pltpu.SemaphoreType.DMA((count,)),
            pltpu.SemaphoreType.DMA((count,)),
            pltpu.SemaphoreType.DMA((2,)),
        ],
        compiler_params=pltpu.CompilerParams(vmem_limit_bytes=VMEM_LIMIT),
        name=name,
    )(*parts, d_both, weighted)


def unpack_weights(traded, stays, passed, ff):
    sides = shares_of(ff)
    rows = traded[0].shape[0]
    (_, one), (begin, two) = sides

    def kernel(*refs):
        traded_refs, stay_refs, passed_refs = refs[0:2], refs[2:4], refs[4:6]
        gate_out, up_out, down_out = refs[6:9]
        for at in range(2):
            of = slice(at * rows, (at + 1) * rows)
            first = traded_refs[at]
            other = (stay_refs[at][...] + passed_refs[at][...].astype(F32)).astype(BF)
            gate_out[of, :one] = first[:, :one]
            gate_out[of, begin:] = other[:, :two]
            up_out[of, :one] = first[:, one : 2 * one]
            up_out[of, begin:] = other[:, two : 2 * two]
            down_out[:one, of] = first[:, 2 * one :].T
            down_out[begin:, of] = other[:, 2 * two :].T

    return pl.pallas_call(
        kernel,
        out_shape=[shape_of(2 * rows, ff), shape_of(2 * rows, ff), shape_of(ff, 2 * rows)],
        in_specs=[VMEM_SPEC] * 6,
        out_specs=[VMEM_SPEC] * 3,
        compiler_params=pltpu.CompilerParams(vmem_limit_bytes=VMEM_LIMIT),
        name="unpack_weights",
    )(*traded, *stays, *passed)


def unpack_rows(place, value):
    rows = value.shape[0]
    depth = value.shape[1] - LANES
    block = depth // 8

    def kernel(place_ref, v_ref, out_ref):
        here = place_ref[0]
        for at, (quarter, half) in enumerate(BLOCKS):
            start = pl.multiple_of(((here ^ quarter) * 2 + half) * block, block)
            out_ref[:, pl.ds(start, block)] = v_ref[:, at * block : (at + 1) * block]

    return pl.pallas_call(
        kernel,
        out_shape=shape_of(rows, depth),
        in_specs=[SMEM_SPEC, VMEM_SPEC],
        out_specs=VMEM_SPEC,
        compiler_params=pltpu.CompilerParams(vmem_limit_bytes=VMEM_LIMIT),
        name="unpack_rows",
    )(place, value)


def summed(got, kept):
    half = got.shape[0] // 2
    stay = kept[:half].astype(F32) + got[:half].astype(F32)
    return stay, (kept[half:].astype(F32) + got[half:].astype(F32)).astype(BF)


def both_swaps(send_x, send_y):
    return lax.optimization_barrier((dp_swap(send_x, 1), dp_swap(send_y, 2)))


def gathered(tokens, cotangent, probs, expert_ids, holder, partner, w_gate, w_up, w_down):
    span = lax.axis_size("expert")
    chips = span // 2
    rows, depth = tokens.shape
    ff = w_gate.shape[2]
    place = lax.axis_index("dp")[None].astype(jnp.int32)
    index = lax.axis_index("expert").astype(jnp.int32)
    everyone = jnp.arange(span, dtype=jnp.int32)
    mate = jnp.sum(jnp.where(everyone == index, partner, 0))
    pair = jnp.stack([index, mate])
    tables = matchings(span)
    chosen = jnp.argmax(jnp.all(jnp.array(tables, jnp.int32) == partner[None, :], axis=1))

    def trade(table):
        pairs = list(enumerate(table))
        return lambda *values: tuple(lax.ppermute(v, "expert", pairs) for v in values)

    branches = [trade(table) for table in tables]

    tile_a, tile_b, packed = pack(
        place, holder, tokens, cotangent, probs.T, expert_ids.T, w_gate[0], w_up[0], w_down[0]
    )
    near_a = dp_swap(tile_a, 1), dp_swap(tile_a, 2)
    first_hop = chip_shift(packed, 1)
    (tile_b,) = lax.switch(chosen, branches, tile_b)
    tile_b, near_a, first_hop = lax.optimization_barrier((tile_b, near_a, first_hop))
    tile_b, far_a = lax.optimization_barrier((tile_b, pass_tiles(*near_a)))
    near_b = dp_swap(tile_b, 1), dp_swap(tile_b, 2)
    hops = [packed, first_hop]
    for _ in range(chips - 2):
        hops.append(chip_shift(hops[-1], 1))
    swapped = [core_swap(one) for one in hops[:-1]]
    near_b, swapped = lax.optimization_barrier((near_b, swapped))
    far_b = pass_tiles(*near_b)
    last, far_b = lax.optimization_barrier((hops[-1], far_b))
    swapped.append(core_swap(last))
    tiles = (tile_a,) + near_a + far_a + (tile_b,) + near_b + far_b
    parts = hops + swapped
    d_both, weighted, near, away = expert_pass(pair, parts, tiles, depth, ff)
    got_rows = core_swap(away)
    sends_a = chunks_of(parts, d_both, weighted, depth, 0, 2, 0, "sent_chunks")
    got_a = both_swaps(*sends_a)
    near, _ = lax.optimization_barrier((near, sends_a[0]))
    both = (near.astype(F32) + got_rows.astype(F32)).astype(BF)
    pieces = [both[s * rows : (s + 1) * rows] for s in range(chips)]
    total = pieces[-1]

    def ring_step(total, s):
        return (pieces[s].astype(F32) + chip_shift(total, -1).astype(F32)).astype(BF)

    left = list(range(chips - 2, -1, -1))
    total = ring_step(total, left.pop(0))
    late, _ = lax.optimization_barrier((weighted, both))
    keeps_a = chunks_of(parts, d_both, late, depth, 2, 2, 0, "kept_chunks")
    late, _ = lax.optimization_barrier((weighted, keeps_a[0]))
    chunks_b = chunks_of(parts, d_both, late, depth, 0, 4, 1, "other_chunks")
    keeps_a, chunks_b, total = lax.optimization_barrier((keeps_a, chunks_b, total))
    keeps = list(keeps_a) + list(chunks_b[2:])
    sends_b = chunks_b[:2]
    if left:
        total = ring_step(total, left.pop(0))
    got_a, total = lax.optimization_barrier((got_a, total))
    stay_low, pass_low = summed(got_a[0], keeps[0])
    stay_high, pass_high = summed(got_a[1], keeps[1])
    passed = dp_swap(pass_low, 2), dp_swap(pass_high, 1)
    for s in left:
        total = ring_step(total, s)
    passed, sends_b = lax.optimization_barrier((passed, sends_b))
    got_b = both_swaps(*sends_b)
    low = (stay_low + passed[0].astype(F32)).astype(BF)
    high = (stay_high + passed[1].astype(F32)).astype(BF)
    low, high, total = lax.optimization_barrier((low, high, total))
    traded = lax.switch(chosen, branches, low, high)
    traded, got_b = lax.optimization_barrier((traded, got_b))
    stay_low, pass_low = summed(got_b[0], keeps[2])
    stay_high, pass_high = summed(got_b[1], keeps[3])
    passed = dp_swap(pass_low, 2), dp_swap(pass_high, 1)
    grad_gate, grad_up, grad_down = unpack_weights(traded, (stay_low, stay_high), passed, ff)

    grad_tokens = unpack_rows(place, total)
    by_slot = total[:, depth : depth + span].astype(F32)
    hits = expert_ids[:, :, None] == holder[None, None, :]
    grad_probs = jnp.sum(jnp.where(hits, by_slot[:, None, :], 0.0), axis=2).astype(BF)
    return grad_tokens, grad_probs, grad_gate[None], grad_up[None], grad_down[None]


def contract_last(left, right):
    return lax.dot_general(
        left, right, (((1,), (1,)), ((), ())), preferred_element_type=jnp.float32
    )


def contract_first(left, right):
    return lax.dot_general(
        left, right, (((0,), (0,)), ((), ())), preferred_element_type=jnp.float32
    )


def move_weights(gate_tile, up_tile, down_tile, partner):
    spread = (
        lax.all_to_all(gate_tile, "expert", split_axis=1, concat_axis=0, tiled=True),
        lax.all_to_all(up_tile, "expert", split_axis=1, concat_axis=0, tiled=True),
        lax.all_to_all(down_tile, "expert", split_axis=1, concat_axis=0, tiled=True),
    )
    chosen = [jnp.take(piece, partner, axis=0) for piece in spread]
    return (
        lax.all_to_all(chosen[0], "expert", split_axis=0, concat_axis=1, tiled=True),
        lax.all_to_all(chosen[1], "expert", split_axis=0, concat_axis=1, tiled=True),
        lax.all_to_all(chosen[2], "expert", split_axis=0, concat_axis=1, tiled=True),
    )


def shards(tokens, cotangent, probs, expert_ids, holder, partner, w_gate, w_up, w_down):
    experts = holder.shape[0]
    span_size = lax.axis_size("expert")
    tok_rows, picks = expert_ids.shape
    pair_count = tok_rows * picks
    capacity = 2 * pair_count // experts
    numbers = jnp.arange(experts, dtype=jnp.int32)
    holder_hits = (holder[None, :] == numbers[:, None]).astype(jnp.int32)
    home_slot = jnp.sum(holder_hits * numbers[None, :], axis=1)
    gate_tile, up_tile, down_tile = move_weights(w_gate, w_up, w_down, partner)
    partner_hits = (home_slot[:, None] == numbers[None, :]).astype(jnp.int32)
    target = jnp.sum(partner_hits * partner[None, :], axis=1)
    full_gate, full_up, full_down = (
        lax.all_gather(gate_tile, "dp", axis=1, tiled=True),
        lax.all_gather(up_tile, "dp", axis=1, tiled=True),
        lax.all_gather(down_tile, "dp", axis=2, tiled=True),
    )
    gate_w = full_gate[0]
    up_w = full_up[0]
    down_w = full_down[0]
    flat_ids = expert_ids.reshape(pair_count)
    onehot = (flat_ids[:, None] == numbers[None, :]).astype(jnp.int32)
    earlier = jnp.cumsum(onehot, axis=0) - onehot
    slot_index = jnp.sum(earlier * onehot, axis=1)
    dest_dev = jnp.sum(onehot * target[None, :], axis=1)
    pair_row = dest_dev * capacity + slot_index
    row_table = (
        jnp.full((span_size * capacity,), pair_count, jnp.int32)
        .at[pair_row]
        .set(jnp.arange(pair_count, dtype=jnp.int32))
    )
    token_of_row = row_table // picks
    zero_row = jnp.zeros((1, tokens.shape[1]), jnp.bfloat16)
    send_x = jnp.concatenate([tokens, zero_row], axis=0)[token_of_row]
    send_dy = jnp.concatenate([cotangent, zero_row], axis=0)[token_of_row]
    send_p = jnp.concatenate([probs.reshape(pair_count), jnp.zeros((1,), jnp.bfloat16)], axis=0)[
        row_table
    ]
    send_scaled = (send_p.astype(jnp.float32)[:, None] * send_dy.astype(jnp.float32)).astype(
        jnp.bfloat16
    )
    recv_x, scaled = (
        lax.all_to_all(send_x, "expert", split_axis=0, concat_axis=0, tiled=True),
        lax.all_to_all(send_scaled, "expert", split_axis=0, concat_axis=0, tiled=True),
    )
    gate_pre = jnp.dot(recv_x, gate_w, preferred_element_type=jnp.float32)
    up_pre = jnp.dot(recv_x, up_w, preferred_element_type=jnp.float32)
    gate_sig = jax.nn.sigmoid(gate_pre)
    hidden = (gate_pre * gate_sig * up_pre).astype(jnp.bfloat16)
    expert_out = jnp.dot(hidden, down_w, preferred_element_type=jnp.float32).astype(jnp.bfloat16)
    d_hidden = contract_last(scaled, down_w)
    d_gate = (d_hidden * up_pre * gate_sig * (1.0 + gate_pre * (1.0 - gate_sig))).astype(
        jnp.bfloat16
    )
    d_up = (d_hidden * gate_pre * gate_sig).astype(jnp.bfloat16)
    pair_grad = (contract_last(d_gate, gate_w) + contract_last(d_up, up_w)).astype(jnp.bfloat16)
    back_out, back_grad = (
        lax.all_to_all(expert_out, "expert", split_axis=0, concat_axis=0, tiled=True),
        lax.all_to_all(pair_grad, "expert", split_axis=0, concat_axis=0, tiled=True),
    )
    row_score = jnp.sum(send_dy.astype(jnp.float32) * back_out.astype(jnp.float32), axis=1).astype(
        jnp.bfloat16
    )
    grad_probs = row_score[pair_row].reshape(tok_rows, picks)
    picked_rows = back_grad[pair_row].reshape(tok_rows, picks, back_grad.shape[1])
    grad_tokens = jnp.sum(picked_rows.astype(jnp.float32), axis=1).astype(jnp.bfloat16)
    shares = (
        lax.psum_scatter(
            contract_first(recv_x, d_gate)[None].astype(jnp.bfloat16),
            "dp",
            scatter_dimension=1,
            tiled=True,
        ).astype(jnp.float32),
        lax.psum_scatter(
            contract_first(recv_x, d_up)[None].astype(jnp.bfloat16),
            "dp",
            scatter_dimension=1,
            tiled=True,
        ).astype(jnp.float32),
        lax.psum_scatter(
            contract_first(hidden, scaled)[None].astype(jnp.bfloat16),
            "dp",
            scatter_dimension=2,
            tiled=True,
        ).astype(jnp.float32),
    )
    grad_gate = shares[0].astype(jnp.bfloat16)
    grad_up = shares[1].astype(jnp.bfloat16)
    grad_down = shares[2].astype(jnp.bfloat16)
    return (grad_tokens, grad_probs, grad_gate, grad_up, grad_down)


def solution(mesh):
    in_specs = (
        P(("dp", "expert"), None),
        P(("dp", "expert"), None),
        P(("dp", "expert"), None),
        P(("dp", "expert"), None),
        P(),
        P(),
        P("expert", "dp", None),
        P("expert", "dp", None),
        P("expert", None, "dp"),
    )
    out_specs = (
        P(("dp", "expert"), None),
        P(("dp", "expert"), None),
        P("expert", "dp", None),
        P("expert", "dp", None),
        P("expert", None, "dp"),
    )
    few = mesh.shape["expert"] <= 8 and mesh.shape["dp"] == 4
    body = gathered if few else shards
    return jax.shard_map(body, mesh=mesh, in_specs=in_specs, out_specs=out_specs, check_vma=False)
```
